32 devices in a mesh: dom: 32 (over z, y, x, core).
Axes of the slice: x: 2, y: 2, z: 4, core: 2. Of those that a mesh axis runs over, the one named last changes fastest.
Arguments:
- positions: float32 [32, 3, 2048], P('dom'), may hold values from -6 to 6
- states: float32 [32, 5, 27, 256], P('dom'), may hold values from -6 to 6
- conn: int32 [32, 27, 256], P('dom'), may hold values from 0 to 2047
- send_nodes: int32 [32, 4, 32], P('dom'), may hold values from 0 to 2047
- recv_nodes: int32 [32, 4, 32], P('dom'), may hold values from 0 to 2047
- send_elems: int32 [32, 4, 16], P('dom'), may hold values from 0 to 255
- neighbours: int32 [32, 6, 256], P('dom'), may hold values from 0 to 319
- live: int32 [32], P('dom'), may hold values from 128 to 256, as said below
- smooth: float32 [27, 27], replicated, may hold values from -1.25 to 1.25
- face_geo: float32 [6, 3, 27], replicated, may hold values from -0.625 to 0.625
- rates: float32 [32, 6, 256], P('dom'), may hold values from 0.1 to 1
- stiff: float32 [27, 27], replicated, may hold values from -1.25 to 1.25
- lift: float32 [6, 27, 27], replicated, may hold values from -1.25 to 1.25
- mass_inv: float32 [27, 27], replicated, may hold values from -1.25 to 1.25
Outputs:
- coords: float32 [32, 3, 2048], P('dom')
- remapped: float32 [32, 5, 27, 256], P('dom')
The draws below stay inside these ranges and needn't reach their ends.
Inputs may be any that keep to these rules, and one draw needn't show every extreme that they name: Elements from live[p] on are padding; at least one partition is full.
All inputs are finite; a program needn't handle non-finite values.
Results may differ from the reference program's by a relative error of at most 0.0001.
Values sent between devices are 32-bit elements; how exact they have to be, the bound alone decides.
A program may use at most 64 MiB of HBM per device.

```python
import math
import jax
import jax.numpy as jnp
from jax import lax

E_DEV = 256
BASIS = 27
FIELDS = 5
FACES = 6
SWEEPS = 3
STEPS = 4
NODES_DEV = 2048
GHOSTS = 16
SHARED = 32
PARTS_SIZE = 32


def draw_live(key, part):
    base = jax.random.randint(key, (PARTS_SIZE,), E_DEV // 2, E_DEV + 1)
    chosen = jax.random.randint(jax.random.fold_in(key, 7), (), 0, PARTS_SIZE)
    return jnp.where(jnp.arange(PARTS_SIZE) == chosen, E_DEV, base).astype(jnp.int32)


def with_ends(array, key, smallest, top_value):
    dims = array.shape
    spot = [jax.random.randint(jax.random.fold_in(key, axis), (), 0, dims[axis]) for axis in range(len(dims))]
    array = array.at[tuple(spot)].set(smallest)
    longest = dims.index(max(dims))
    spot[longest] = (spot[longest] + 1) % dims[longest]
    return array.at[tuple(spot)].set(top_value)


def level_of(key, dims, shards, low, high):
    def one(dim, blocks):
        steps = jax.random.uniform(jax.random.fold_in(jax.random.fold_in(key, 6), dim), (blocks,), jnp.float32, low / len(shards), high / len(shards))
        return jnp.repeat(jnp.exp(steps), dims[dim] // blocks).reshape((-1,) + (1,) * (len(dims) - dim - 1))

    level = one(*shards[0])
    for cut in shards[1:]:
        level = level * one(*cut)
    return level


def noise(stream_key, dims, scale, most, pieces=(), held_as=jnp.bfloat16):
    factor_of = level_of(stream_key, dims, pieces, -0.22, 0.18) if pieces else 1.0
    result = jax.random.normal(stream_key, dims, jnp.float32) * scale * factor_of
    return jnp.minimum(jnp.maximum(result, -most), most).astype(held_as)


def setup_inputs(seed: int = 0) -> dict:
    arg_keys = jax.random.split(jax.random.key(seed), 15)
    return {
        "positions": noise(arg_keys[0], (PARTS_SIZE, 3, NODES_DEV), 1.0, 6.0, ((0, 32),), jnp.float32),
        "states": noise(arg_keys[1], (PARTS_SIZE, FIELDS, BASIS, E_DEV), 1.0, 6.0, ((0, 32),), jnp.float32),
        "conn": with_ends(jax.random.randint(arg_keys[2], (PARTS_SIZE, BASIS, E_DEV), 0, NODES_DEV), jax.random.fold_in(arg_keys[2], 1), 0, NODES_DEV - 1).astype(jnp.int32),
        "send_nodes": with_ends(jax.random.randint(arg_keys[3], (PARTS_SIZE, 4, SHARED), 0, NODES_DEV), jax.random.fold_in(arg_keys[3], 1), 0, NODES_DEV - 1).astype(jnp.int32),
        "recv_nodes": with_ends(jax.random.randint(arg_keys[4], (PARTS_SIZE, 4, SHARED), 0, NODES_DEV), jax.random.fold_in(arg_keys[4], 1), 0, NODES_DEV - 1).astype(jnp.int32),
        "send_elems": with_ends(jax.random.randint(arg_keys[5], (PARTS_SIZE, 4, GHOSTS), 0, E_DEV), jax.random.fold_in(arg_keys[5], 1), 0, E_DEV - 1).astype(jnp.int32),
        "neighbours": with_ends(jax.random.randint(arg_keys[6], (PARTS_SIZE, FACES, E_DEV), 0, E_DEV + 4 * GHOSTS), jax.random.fold_in(arg_keys[6], 1), 0, (E_DEV + 4 * GHOSTS) - 1).astype(jnp.int32),
        "live": draw_live(jax.random.fold_in(arg_keys[14], 71), 0),
        "smooth": noise(arg_keys[8], (BASIS, BASIS), BASIS ** -0.5, 1.25, (), jnp.float32),
        "face_geo": noise(arg_keys[9], (FACES, 3, BASIS), (3 * BASIS) ** -0.5, 0.625, (), jnp.float32),
        "rates": jnp.clip(jnp.exp(math.log(1.0) - 2.3025851 * jax.random.uniform(arg_keys[10], (PARTS_SIZE, FACES, E_DEV), jnp.float32) ** level_of(arg_keys[10], (PARTS_SIZE, FACES, E_DEV), ((0, 32),), -0.2, 0.2)), 0.1, 1.0),
        "stiff": noise(arg_keys[11], (BASIS, BASIS), BASIS ** -0.5, 1.25, (), jnp.float32),
        "lift": noise(arg_keys[12], (FACES, BASIS, BASIS), BASIS ** -0.5, 1.25, (), jnp.float32),
        "mass_inv": noise(arg_keys[13], (BASIS, BASIS), BASIS ** -0.5, 1.25, (), jnp.float32),
    }


relax_factor = 0.5
cfl_number = 0.4
highest = lax.Precision.HIGHEST


def neighbour_offsets(parts):
    stride = max(parts // 8, 1)
    return (1, -1, stride, -stride)


def node_counts(connect, receive, mask, nodes):
    weights = jnp.broadcast_to(mask[None, :], connect.shape).reshape(-1)
    counted = jnp.zeros((nodes,), jnp.float32).at[connect.reshape(-1)].add(weights)
    counted = counted.at[receive.reshape(-1)].add(jnp.ones((receive.size,), jnp.float32))
    return jnp.maximum(counted, 1.0)


def assemble(coords, connect, mask, smooth):
    corner = coords[:, connect]
    smoothed = jnp.einsum('ab,cbe->cae', smooth, corner, precision=highest) * mask[None, None, :]
    flat = smoothed.reshape(coords.shape[0], -1)
    return jnp.zeros(coords.shape, jnp.float32).at[:, connect.reshape(-1)].add(flat)


def face_rates(moved, connect, face_geo, rates, mask):
    corner = moved[:, connect]
    projected = jnp.einsum('fca,cae->fe', face_geo, corner, precision=highest)
    return rates * (1.0 + 0.5 * jnp.tanh(projected)) * mask[None, :]


def advance(values, extended, neighbour, rate, mask, step_size, stiff, lift, mass_inv):
    flux = jnp.einsum('ab,vbe->vae', stiff, values, precision=highest)
    for face in range(6):
        other = jnp.take(extended, neighbour[face], axis=2)
        flux = flux + rate[face][None, None, :] * jnp.einsum('ab,vbe->vae', lift[face], other - values, precision=highest)
    change = jnp.einsum('ab,vbe->vae', mass_inv, flux, precision=highest)
    return values + step_size * change * mask[None, None, :]


def reference(positions, states, conn, send_nodes, recv_nodes, send_elems, neighbours, live, smooth, face_geo, rates, stiff, lift, mass_inv):
    parts = positions.shape[0]
    shifts = neighbour_offsets(parts)
    elems = conn.shape[-1]
    nodes = positions.shape[-1]
    mask = (jnp.arange(elems)[None, :] < live[:, None]).astype(jnp.float32)
    counts = lax.map(lambda item: node_counts(item[0], item[1], item[2], nodes), (conn, recv_nodes, mask))
    coords = positions
    for sweep in range(SWEEPS):
        summed = lax.map(lambda item: assemble(item[0], item[1], item[2], smooth), (coords, conn, mask))
        total = summed
        for k in range(4):
            picked = jax.vmap(lambda rows, index: rows[:, index])(summed, send_nodes[:, k])
            arrived = jnp.roll(picked, shifts[k], axis=0)
            total = jax.vmap(lambda acc, index, add: acc.at[:, index].add(add))(total, recv_nodes[:, k], arrived)
        coords = coords + relax_factor * (total / counts[:, None, :] - coords)
    moved = coords - positions
    rate = lax.map(lambda item: face_rates(item[0], item[1], face_geo, item[2], item[3]), (moved, conn, rates, mask))
    step_size = cfl_number / jnp.max(jnp.sum(rate, axis=1))
    values = states
    for step in range(STEPS):
        ghosts = []
        for k in range(4):
            picked = jax.vmap(lambda vals, index: vals[:, :, index])(values, send_elems[:, k])
            ghosts.append(jnp.roll(picked, shifts[k], axis=0))
        extended = jnp.concatenate([values] + ghosts, axis=3)
        values = lax.map(lambda item: advance(item[0], item[1], item[2], item[3], item[4], step_size, stiff, lift, mass_inv), (values, extended, neighbours, rate, mask))
    return coords, values
```

```python
import functools
import math

import jax
import jax.numpy as jnp
from jax import lax
from jax.experimental import pallas as pl
from jax.experimental.pallas import tpu as pltpu
from jax.sharding import PartitionSpec as P

SWEEPS = 3
STEPS = 4
CFL = 0.4
F32 = jnp.float32
BF16 = jnp.bfloat16
HIGHEST = lax.Precision.HIGHEST
MESH = pl.DeviceIdType.MESH
LANES = 128
ROWS = 32
RADIX = 8


def rounds_of(parts):
    found, stride = [], 1
    while parts > 1:
        radix = max(r for r in range(1, RADIX + 1) if parts % r == 0)
        if radix == 1:
            radix = parts
        found.append((radix, stride))
        stride *= radix
        parts //= radix
    return found


def pick(table, index):
    return jnp.take_along_axis(table, index, axis=1, mode="promise_in_bounds")


def split(x):
    high = x.astype(BF16)
    low = (x - high.astype(F32)).astype(BF16)
    return high, low


def mm(a, b):
    return jnp.dot(a, b, preferred_element_type=F32)


def mm3(a, b):
    high, low = split(b)
    return mm(a[0], high) + (mm(a[1], high) + mm(a[0], low))


def mm_nt(a, b):
    return lax.dot_general(a, b, (((1,), (1,)), ((), ())), preferred_element_type=F32)


def iota(shape, dim):
    return lax.broadcasted_iota(jnp.int32, shape, dim)


def kernel(
    parts, shifts, rounds,
    basis, elems, fields, faces, nodes,
    pos_any, states_any, conn_any, send_nodes_any, recv_nodes_any, send_elems_any, neighbours_any, live,
    smooth_any, face_geo_any, rates_any, stiff_any, lift_any, mass_inv_any,
    out_c, out_u,
    x0_ref, states, conn, send_nodes, recv_nodes, send_elems, neighbours,
    smooth, face_geo, rates, stiff, lift, mass_inv, in_sem,
    x_ref, s_ref, lo_ref, hi_ref, y_ref, z_ref, b_ref, rb_ref,
    u_ref, nb_ref, rate_ref, pad_ref, fg_ref, w_ref, idx_ref,
    v_send, v_recv, g_send, g_recv, m_send, m_recv,
    vs_sem, vr_sem, gs_sem, gr_sem, ms_sem, mr_sem,
):
    me = lax.axis_index("dom")
    groups = nodes // LANES
    halves = elems // LANES
    shared = send_nodes.shape[1]
    ghosts = send_elems.shape[1]
    slots = LANES // ghosts

    sources = (
        conn_any, pos_any, states_any, send_elems_any, send_nodes_any, recv_nodes_any, smooth_any,
        neighbours_any, rates_any, face_geo_any, mass_inv_any, stiff_any, lift_any,
    )
    places = (
        conn, x0_ref, states, send_elems, send_nodes, recv_nodes, smooth,
        neighbours, rates, face_geo, mass_inv, stiff, lift,
    )
    loads = [
        pltpu.make_async_copy(a, b, in_sem.at[i]) for i, (a, b) in enumerate(zip(sources, places))
    ]
    for one in loads:
        one.start()

    partners = []
    for radix, stride in rounds:
        digit = lax.rem(me // stride, radix)
        partners.append(
            [me + (lax.rem(digit + j, radix) - digit) * stride for j in range(1, radix)]
        )
    targets = [lax.rem(me + o + parts, parts) for o in shifts]

    barrier = pltpu.get_barrier_semaphore()
    greeted = targets + [t for one in partners for t in one]
    for t in greeted:
        pl.semaphore_signal(barrier, inc=1, device_id=(t,), device_id_type=MESH)

    u_ref[0] = jnp.zeros(u_ref.shape[1:], F32)
    for one in loads:
        one.wait()
    for v in range(fields):
        for h in range(halves):
            u_ref[0, v * ROWS : v * ROWS + basis, h * LANES : (h + 1) * LANES] = states[v * basis : (v + 1) * basis, h, :]

    lane = iota((8, LANES), 1)
    row = iota((8, LANES), 0)
    idx_ref[...] = jnp.zeros(idx_ref.shape, jnp.int32)
    idx_ref[0:4, 0:shared] = send_nodes[...]
    idx_ref[8:12, 0:shared] = recv_nodes[...]
    idx_ref[16:20, 0:ghosts] = send_elems[...]

    def flat(block):
        spread = pick(block, lax.rem(lane, shared))
        kept = jnp.where(lane // shared == row, spread, 0)
        return jnp.sum(kept, axis=0, keepdims=True)

    sent_nodes = flat(idx_ref[0:8, :])
    got_nodes = flat(idx_ref[8:16, :])
    idx_ref[16:24, :] = pick(idx_ref[16:24, :], lax.rem(lane, ghosts))

    slot_of = iota((ROWS, LANES), 1) // ghosts

    def pack_ghosts(step):
        for k in range(4):
            which = jnp.broadcast_to(idx_ref[16 + k : 17 + k, :], (ROWS, LANES))
            low = which & (LANES - 1)
            far = which >> 7
            tile = jnp.zeros((ROWS, LANES), F32)
            for v in range(fields):
                got = pick(u_ref[step, v * ROWS : (v + 1) * ROWS, 0:LANES], low)
                for h in range(1, halves):
                    other = pick(u_ref[step, v * ROWS : (v + 1) * ROWS, h * LANES : (h + 1) * LANES], low)
                    got = jnp.where(far == h, other, got)
                tile = jnp.where(slot_of == (v + k) % slots, got, tile)
            g_send[step, k] = tile

    def ghost_copy(step, k):
        return pltpu.make_async_remote_copy(
            src_ref=g_send.at[step, k], dst_ref=g_recv.at[step, k],
            send_sem=gs_sem.at[step, k], recv_sem=gr_sem.at[step, k],
            device_id=(targets[k],), device_id_type=MESH,
        )

    def node_copy(sweep, k):
        return pltpu.make_async_remote_copy(
            src_ref=v_send.at[sweep], dst_ref=v_recv.at[sweep, k],
            send_sem=vs_sem.at[sweep, k], recv_sem=vr_sem.at[sweep, k],
            device_id=(targets[k],), device_id_type=MESH,
        )

    def most_copy(r, j):
        at = sum(len(p) for p in partners[:r]) + j
        return pltpu.make_async_remote_copy(
            src_ref=m_send.at[r], dst_ref=m_recv.at[at],
            send_sem=ms_sem.at[at], recv_sem=mr_sem.at[at],
            device_id=(partners[r][j],), device_id_type=MESH,
        )

    pack_ghosts(0)

    x_ref[...] = x0_ref[...]
    s_ref[...] = jnp.zeros(s_ref.shape, F32)

    alive = (iota((1, elems), 1) < live[0])
    lo_ref[...] = jnp.zeros(lo_ref.shape, jnp.int32)
    hi_ref[...] = jnp.zeros(hi_ref.shape, jnp.int32)
    for h in range(halves):
        part = conn[:, h, :]
        lo_ref[0:basis, h * LANES : (h + 1) * LANES] = part & (LANES - 1)
        hi_ref[0:basis, h * LANES : (h + 1) * LANES] = part >> 7

    sub_lo = iota((LANES, elems), 0)
    sub_hi = iota((groups, elems), 0)
    one_lo, one_hi = jnp.float32(1.0), jnp.float32(1.0)
    for a in range(basis):
        at = pl.ds(a * elems, elems)
        b_ref[:, at] = jnp.where(sub_lo == lo_ref[a : a + 1, :], one_lo, 0.0).astype(BF16)
        z_ref[0:groups, at] = jnp.where(
            jnp.where(alive, hi_ref[a : a + 1, :], groups) == sub_hi, one_hi, 0.0
        ).astype(BF16)
    got_lo, got_hi = got_nodes & (LANES - 1), got_nodes >> 7
    rb_ref[...] = jnp.where(iota((LANES, LANES), 0) == got_lo, one_lo, 0.0).astype(BF16)
    got_mask = iota((groups, LANES), 0) == got_hi
    count = mm_nt(z_ref[0:groups, :], b_ref[...])
    count = count + mm_nt(jnp.where(got_mask, one_hi, 0.0).astype(BF16), rb_ref[...])
    half_inv = 0.5 / jnp.maximum(count, 1.0)
    half_inv = jnp.concatenate([half_inv] * 3, axis=0)

    pl.semaphore_wait(barrier, len(greeted))
    for k in range(4):
        ghost_copy(0, k).start()

    pad_ref[...] = jnp.zeros(pad_ref.shape, F32)
    for i in range(faces + 1):
        matrix = stiff[...] if i == 0 else lift[i - 1]
        pad_ref[i * ROWS : i * ROWS + basis, 0:basis] = jnp.dot(
            mass_inv[...], matrix, precision=HIGHEST, preferred_element_type=F32
        )
    wide = []
    for first in range(0, faces + 1, 4):
        total = None
        for i in range(first, min(first + 4, faces + 1)):
            block = pad_ref[i * ROWS : (i + 1) * ROWS, :]
            if i > first:
                block = pltpu.roll(block, ROWS * (i - first), 1)
            total = block if total is None else total + block
        wide.append(total)
    w_high, w_low = split(jnp.concatenate(wide, axis=1))
    w_ref[0:ROWS, :] = w_high
    w_ref[ROWS : 2 * ROWS, :] = w_low
    pad_ref[0:ROWS, :] = jnp.zeros((ROWS, LANES), F32)
    pad_ref[0:basis, 0:basis] = smooth[...]
    smooth_parts = split(pad_ref[0:ROWS, 0:ROWS])
    fg_ref[...] = jnp.zeros(fg_ref.shape, F32)
    for c in range(3):
        fg_ref[c * 8 : c * 8 + faces, 0:basis] = face_geo[:, c, :]

    def corners(table):
        result = []
        for c in range(3):
            cols = []
            for h in range(halves):
                low = lo_ref[:, h * LANES : (h + 1) * LANES]
                high = hi_ref[:, h * LANES : (h + 1) * LANES]
                value = jnp.zeros((ROWS, LANES), F32)
                for g in range(groups):
                    r = c * groups + g
                    source = jnp.broadcast_to(table[r : r + 1, :], (ROWS, LANES))
                    value = jnp.where(high == g, pick(source, low), value)
                cols.append(value)
            result.append(jnp.concatenate(cols, axis=1))
        return result

    s_low = jnp.broadcast_to(sent_nodes & (LANES - 1), (8, LANES))
    s_high = jnp.broadcast_to(sent_nodes >> 7, (8, LANES))

    for sweep in range(SWEEPS):
        near = corners(x_ref)
        for c in range(3):
            y = mm3(smooth_parts, near[c])
            y_high = y.astype(BF16).astype(F32)
            y_ref[c * ROWS : (c + 1) * ROWS, :] = y_high
            y_ref[(3 + c) * ROWS : (4 + c) * ROWS, :] = y - y_high
        for a in range(basis):
            at = pl.ds(a * elems, elems)
            chosen = jnp.where(alive, hi_ref[a : a + 1, :], groups) == sub_hi
            for i in range(6):
                z_ref[i * groups : (i + 1) * groups, at] = jnp.where(
                    chosen, y_ref[i * ROWS + a : i * ROWS + a + 1, :], 0.0
                ).astype(BF16)
        both = mm_nt(z_ref[...], b_ref[...])
        sums = both[0 : 3 * groups] + both[3 * groups :]
        for c in range(3):
            for g in range(groups):
                r = c * groups + g
                s_ref[g * 8 + c : g * 8 + c + 1, :] = sums[r : r + 1, :]
        picked = jnp.zeros((8, LANES), F32)
        for g in range(groups):
            picked = jnp.where(s_high == g, pick(s_ref[g * 8 : g * 8 + 8, :], s_low), picked)
        v_send[sweep] = jnp.where(row < 3, picked, 0.0)
        for k in range(4):
            node_copy(sweep, k).start()
        for k in range(4):
            node_copy(sweep, k).wait_recv()
        arrived = v_recv[sweep, 0]
        for k in range(1, 4):
            arrived = jnp.where(lane // shared == k, v_recv[sweep, k], arrived)
        arr_high = arrived.astype(BF16).astype(F32)
        arr_low = arrived - arr_high
        pieces = [
            jnp.where(got_mask, part[c : c + 1, :], 0.0).astype(BF16)
            for part in (arr_high, arr_low) for c in range(3)
        ]
        both = mm_nt(jnp.concatenate(pieces, axis=0), rb_ref[...])
        sums = sums + (both[0 : 3 * groups] + both[3 * groups :])
        x_ref[...] = 0.5 * x_ref[...] + sums * half_inv

    out_c[...] = x_ref[...]

    x_ref[...] = x_ref[...] - x0_ref[...]
    near = corners(x_ref)
    projected = jnp.zeros((8, elems), F32)
    for c in range(3):
        projected = projected + mm3(split(fg_ref[c * 8 : c * 8 + 8, 0:ROWS]), near[c])
    base = jnp.concatenate([rates[:, h, :] for h in range(halves)], axis=1)
    rate = base * (1.0 + 0.5 * jnp.tanh(projected[0:faces])) * jnp.where(alive, 1.0, 0.0)
    rate_ref[0:faces, :] = rate
    most = jnp.max(jnp.sum(rate, axis=0, keepdims=True), axis=1, keepdims=True)
    m_send[0] = jnp.broadcast_to(most, (1, LANES))
    for j in range(len(partners[0]) if rounds else 0):
        most_copy(0, j).start()

    def gather_local(step):
        for v in range(fields):
            for h in range(halves):
                for f in range(faces):
                    which = jnp.broadcast_to(
                        neighbours[f, h : h + 1, :], (ROWS, LANES)
                    )
                    low, far = which & (LANES - 1), which >> 7
                    got = pick(u_ref[step, v * ROWS : (v + 1) * ROWS, 0:LANES], low)
                    for s in range(1, halves):
                        other = pick(u_ref[step, v * ROWS : (v + 1) * ROWS, s * LANES : (s + 1) * LANES], low)
                        got = jnp.where(far == s, other, got)
                    r = (v * faces + f) * ROWS
                    nb_ref[r : r + ROWS, h * LANES : (h + 1) * LANES] = got

    def change_of(step, v):
        ghost = g_recv[step, 0]
        for k in range(1, 4):
            ghost = jnp.where(slot_of == (v + k) % slots, g_recv[step, k], ghost)
        u = u_ref[step, v * ROWS : (v + 1) * ROWS, :]
        stack = [u]
        for f in range(faces):
            cols = []
            r = (v * faces + f) * ROWS
            for h in range(halves):
                which = jnp.broadcast_to(
                    neighbours[f, h : h + 1, :], (ROWS, LANES)
                )
                got = pick(ghost, (which + ghosts * v) & (LANES - 1))
                cols.append(jnp.where(which >= elems, got, nb_ref[r : r + ROWS, h * LANES : (h + 1) * LANES]))
            stack.append(rate_ref[f : f + 1, :] * (jnp.concatenate(cols, axis=1) - u))
        high, low = split(jnp.concatenate(stack, axis=0))
        depth = (faces + 1) * ROWS
        first = mm(w_ref[:, 0:depth], high)
        return first[0:ROWS] + (first[ROWS:] + mm(w_ref[0:ROWS, 0:depth], low))

    def finish_round(r, most):
        at = sum(len(p) for p in partners[:r])
        tile = m_send[r]
        for j in range(len(partners[r])):
            most_copy(r, j).wait_recv()
            tile = jnp.maximum(tile, m_recv[at + j])
        most = tile[0:1, 0:1]
        if r + 1 < len(partners):
            m_send[r + 1] = jnp.broadcast_to(most, (1, LANES))
            for j in range(len(partners[r + 1])):
                most_copy(r + 1, j).start()
        return most

    keep = jnp.where(alive, 1.0, 0.0)
    for step in range(STEPS):
        if step > 0:
            pack_ghosts(step)
            for k in range(4):
                ghost_copy(step, k).start()
        gather_local(step)
        for k in range(4):
            ghost_copy(step, k).wait_recv()
        if 0 < step <= len(partners):
            most = finish_round(step - 1, most)
        for v in range(fields):
            u_ref[step + 1, v * ROWS : (v + 1) * ROWS, :] = keep * change_of(step, v)
    for r in range(STEPS - 1, len(partners)):
        most = finish_round(r, most)
    scale = jnp.broadcast_to(CFL / most, (ROWS, elems))
    for v in range(fields):
        term = [u_ref[k, v * ROWS : (v + 1) * ROWS, :] for k in range(STEPS + 1)]
        new = term[STEPS]
        for k in range(STEPS - 1, -1, -1):
            new = math.comb(STEPS, k) * term[k] + scale * new
        for h in range(halves):
            out_u[v * basis : (v + 1) * basis, h, :] = new[
                0:basis, h * LANES : (h + 1) * LANES
            ]

    for sweep in range(SWEEPS):
        for k in range(4):
            node_copy(sweep, k).wait_send()
    for step in range(STEPS):
        for k in range(4):
            ghost_copy(step, k).wait_send()
    for r, one in enumerate(partners):
        for j in range(len(one)):
            most_copy(r, j).wait_send()


def hand_over(coords, remapped, out_c, out_u, held_c, held_u, sem):
    half = remapped.shape[0] // 2
    parts = [(coords, held_c, out_c)]
    for at in (pl.ds(0, half), pl.ds(half, remapped.shape[0] - half)):
        parts.append((remapped.at[at], held_u.at[at], out_u.at[at]))
    reads = [pltpu.make_async_copy(a, b, sem.at[0, i]) for i, (a, b, _) in enumerate(parts)]
    writes = [pltpu.make_async_copy(b, c, sem.at[1, i]) for i, (_, b, c) in enumerate(parts)]
    for one in reads:
        one.start()
    for read, write in zip(reads, writes):
        read.wait()
        write.start()
    for one in writes:
        one.wait()


def on_device(*args):
    pos, states, conn = args[:3]
    parts = lax.axis_size("dom")
    w = max(parts // 8, 1)
    shifts = (1, -1, w, -w)
    rounds = rounds_of(parts)
    total = sum(r - 1 for r, _ in rounds)
    basis, elems = conn.shape[1:]
    fields, faces = states.shape[1], args[6].shape[1]
    groups = pos.shape[2] // LANES
    nodes = pos.shape[2]
    halves = elems // LANES
    flat = list(args)
    for i, rows in ((0, 3 * groups), (1, fields * basis * halves), (2, basis * halves), (6, faces * halves), (10, faces * halves)):
        flat[i] = args[i].reshape(rows, LANES) if i == 0 else args[i].reshape(rows // halves, halves, LANES)
    for i in (3, 4, 5):
        flat[i] = args[i][0]
    vmem = pl.BlockSpec(memory_space=pltpu.VMEM)
    smem = pl.BlockSpec(memory_space=pltpu.SMEM)
    hbm = pl.BlockSpec(memory_space=pl.ANY)
    specs = [smem if i == 7 else hbm for i in range(len(args))]
    held = [pltpu.VMEM(a.shape, a.dtype) for i, a in enumerate(flat) if i != 7]
    scratch = held + [
        pltpu.SemaphoreType.DMA((len(held),)),
        pltpu.VMEM((3 * groups, LANES), F32),
        pltpu.VMEM((8 * groups, LANES), F32),
        pltpu.VMEM((ROWS, elems), jnp.int32),
        pltpu.VMEM((ROWS, elems), jnp.int32),
        pltpu.VMEM((6 * ROWS, elems), F32),
        pltpu.VMEM((6 * groups, basis * elems), BF16),
        pltpu.VMEM((LANES, basis * elems), BF16),
        pltpu.VMEM((LANES, LANES), BF16),
        pltpu.VMEM((STEPS + 1, fields * ROWS, elems), F32),
        pltpu.VMEM((fields * faces * ROWS, elems), F32),
        pltpu.VMEM((8, elems), F32),
        pltpu.VMEM(((faces + 1) * ROWS, LANES), F32),
        pltpu.VMEM((24, LANES), F32),
        pltpu.VMEM((2 * ROWS, 2 * LANES), BF16),
        pltpu.VMEM((24, LANES), jnp.int32),
        pltpu.VMEM((SWEEPS, 8, LANES), F32),
        pltpu.VMEM((SWEEPS, 4, 8, LANES), F32),
        pltpu.VMEM((STEPS, 4, ROWS, LANES), F32),
        pltpu.VMEM((STEPS, 4, ROWS, LANES), F32),
        pltpu.VMEM((max(len(rounds), 1), 1, LANES), F32),
        pltpu.VMEM((max(total, 1), 1, LANES), F32),
        pltpu.SemaphoreType.DMA((SWEEPS, 4)),
        pltpu.SemaphoreType.DMA((SWEEPS, 4)),
        pltpu.SemaphoreType.DMA((STEPS, 4)),
        pltpu.SemaphoreType.DMA((STEPS, 4)),
        pltpu.SemaphoreType.DMA((max(total, 1),)),
        pltpu.SemaphoreType.DMA((max(total, 1),)),
    ]
    coords, remapped = pl.pallas_call(
        functools.partial(kernel, parts, shifts, rounds, basis, elems, fields, faces, nodes),
        out_shape=(
            jax.ShapeDtypeStruct((3 * groups, LANES), F32),
            jax.ShapeDtypeStruct((fields * basis, halves, LANES), F32),
        ),
        in_specs=specs,
        out_specs=(vmem, vmem),
        scratch_shapes=scratch,
        compiler_params=pltpu.CompilerParams(
            collective_id=0, has_side_effects=True, vmem_limit_bytes=60 * 1024 * 1024
        ),
    )(*flat)
    coords, remapped = pl.pallas_call(
        hand_over,
        out_shape=(
            jax.ShapeDtypeStruct(coords.shape, F32),
            jax.ShapeDtypeStruct(remapped.shape, F32),
        ),
        in_specs=[hbm, hbm],
        out_specs=(hbm, hbm),
        scratch_shapes=[
            pltpu.VMEM(coords.shape, F32),
            pltpu.VMEM(remapped.shape, F32),
            pltpu.SemaphoreType.DMA((2, 3)),
        ],
        compiler_params=pltpu.CompilerParams(vmem_limit_bytes=60 * 1024 * 1024),
    )(coords, remapped)
    return coords.reshape(pos.shape), remapped.reshape(states.shape)


def solution(mesh):
    dom = lambda rank: P("dom", *([None] * (rank - 1)))
    in_specs = (
        dom(3), dom(4), dom(3), dom(3), dom(3), dom(3), dom(3), P("dom"),
        P(), P(), dom(3), P(), P(), P(),
    )
    return jax.shard_map(
        on_device, mesh=mesh, in_specs=in_specs, out_specs=(dom(3), dom(4)), check_vma=False
    )
```

```python
import functools
import math

import jax
import jax.numpy as jnp
from jax import lax
from jax.experimental import pallas as pl
from jax.experimental.pallas import tpu as pltpu
from jax.sharding import PartitionSpec as P

SWEEPS = 3
STEPS = 4
CFL = 0.4
F32 = jnp.float32
BF16 = jnp.bfloat16
HIGHEST = lax.Precision.HIGHEST
MESH = pl.DeviceIdType.MESH
LANES = 128
ROWS = 32
RADIX = 8


def rounds_of(parts):
    found, stride = [], 1
    while parts > 1:
        radix = max(r for r in range(1, RADIX + 1) if parts % r == 0)
        if radix == 1:
            radix = parts
        found.append((radix, stride))
        stride *= radix
        parts //= radix
    return found


def pick(table, index):
    return jnp.take_along_axis(table, index, axis=1, mode="promise_in_bounds")


def split(x):
    high = x.astype(BF16)
    low = (x - high.astype(F32)).astype(BF16)
    return high, low


def mm(a, b):
    return jnp.dot(a, b, preferred_element_type=F32)


def mm3(a, b):
    high, low = split(b)
    return mm(a[0], high) + (mm(a[1], high) + mm(a[0], low))


def mm_nt(a, b):
    return lax.dot_general(a, b, (((1,), (1,)), ((), ())), preferred_element_type=F32)


def iota(shape, dim):
    return lax.broadcasted_iota(jnp.int32, shape, dim)


def kernel(
    parts, shifts, rounds,
    basis, elems, fields, faces, nodes,
    pos_any, states_any, conn_any, send_nodes_any, recv_nodes_any, send_elems_any, neighbours_any, live,
    smooth_any, face_geo_any, rates_any, stiff_any, lift_any, mass_inv_any,
    out_c, out_u,
    x0_ref, states, conn, send_nodes, recv_nodes, send_elems, neighbours,
    smooth, face_geo, rates, stiff, lift, mass_inv, in_sem,
    x_ref, s_ref, lo_ref, hi_ref, y_ref, z_ref, b_ref, rb_ref,
    u_ref, nb_ref, rate_ref, pad_ref, fg_ref, w_ref, idx_ref,
    mv_ref, yr_ref, yw_ref, gs_ref, sl_ref, st_ref, gt_ref, nl_ref, nbs_ref, rs_ref, nbp_ref,
    v_send, v_recv, g_send, g_recv, m_send, m_recv,
    vs_sem, vr_sem, gs_sem, gr_sem, ms_sem, mr_sem,
):
    me = lax.axis_index("dom")
    groups = nodes // LANES
    halves = elems // LANES
    shared = send_nodes.shape[1]
    ghosts = send_elems.shape[1]
    slots = LANES // ghosts

    sources = (
        conn_any, pos_any, states_any, send_elems_any, send_nodes_any, recv_nodes_any, smooth_any,
        neighbours_any, rates_any, face_geo_any, mass_inv_any, stiff_any, lift_any,
    )
    places = (
        conn, x0_ref, states, send_elems, send_nodes, recv_nodes, smooth,
        neighbours, rates, face_geo, mass_inv, stiff, lift,
    )
    loads = [
        pltpu.make_async_copy(a, b, in_sem.at[i]) for i, (a, b) in enumerate(zip(sources, places))
    ]
    for one in loads:
        one.start()

    partners = []
    for radix, stride in rounds:
        digit = lax.rem(me // stride, radix)
        partners.append(
            [me + (lax.rem(digit + j, radix) - digit) * stride for j in range(1, radix)]
        )
    targets = [lax.rem(me + o + parts, parts) for o in shifts]

    barrier = pltpu.get_barrier_semaphore()
    greeted = targets + [t for one in partners for t in one]
    for t in greeted:
        pl.semaphore_signal(barrier, inc=1, device_id=(t,), device_id_type=MESH)

    def node_copy(sweep, k):
        return pltpu.make_async_remote_copy(
            src_ref=v_send.at[sweep], dst_ref=v_recv.at[sweep, k],
            send_sem=vs_sem.at[sweep, k], recv_sem=vr_sem.at[sweep, k],
            device_id=(targets[k],), device_id_type=MESH,
        )

    def ghost_copy(step, k):
        return pltpu.make_async_remote_copy(
            src_ref=g_send.at[step, k], dst_ref=g_recv.at[step, k],
            send_sem=gs_sem.at[step, k], recv_sem=gr_sem.at[step, k],
            device_id=(targets[k],), device_id_type=MESH,
        )

    def most_copy(r, j):
        at = sum(len(p) for p in partners[:r]) + j
        return pltpu.make_async_remote_copy(
            src_ref=m_send.at[r], dst_ref=m_recv.at[at],
            send_sem=ms_sem.at[at], recv_sem=mr_sem.at[at],
            device_id=(partners[r][j],), device_id_type=MESH,
        )

    lane = iota((8, LANES), 1)
    row = iota((8, LANES), 0)
    slot_of = iota((ROWS, LANES), 1) // ghosts
    tiles = (fields + 1) // 2

    idx_ref[...] = jnp.zeros(idx_ref.shape, jnp.int32)
    lo_ref[...] = jnp.zeros(lo_ref.shape, jnp.int32)
    hi_ref[...] = jnp.zeros(hi_ref.shape, jnp.int32)
    s_ref[...] = jnp.zeros(s_ref.shape, F32)
    u_ref[0] = jnp.zeros(u_ref.shape[1:], F32)
    yr_ref[...] = jnp.zeros(yr_ref.shape, F32)
    pad_ref[...] = jnp.zeros(pad_ref.shape, F32)
    fg_ref[...] = jnp.zeros(fg_ref.shape, F32)
    nbp_ref[...] = jnp.zeros(nbp_ref.shape, jnp.int32)
    rate_ref[...] = jnp.zeros(rate_ref.shape, F32)
    alive = iota((1, elems), 1) < live[0]
    for one in loads:
        one.wait()

    pad_ref[0:basis, 0:basis] = smooth[...]
    smooth_parts = split(pad_ref[0:ROWS, 0:ROWS])
    idx_ref[0:4, 0:shared] = send_nodes[...]
    idx_ref[8:12, 0:shared] = recv_nodes[...]
    idx_ref[16:20, 0:ghosts] = send_elems[...]

    def flat(block, width, count):
        spread = pick(block, lax.rem(lane, width))
        kept = jnp.where(lax.rem(lane // width, count) == row, spread, 0)
        return jnp.sum(kept, axis=0, keepdims=True)

    sent_nodes = flat(idx_ref[0:8, :], shared, 4)
    got_nodes = flat(idx_ref[8:16, :], shared, 4)

    for h in range(halves):
        part = conn[:, h, :]
        lo_ref[0:basis, h * LANES : (h + 1) * LANES] = part & (LANES - 1)
        hi_ref[0:basis, h * LANES : (h + 1) * LANES] = part >> 7

    sub_lo = iota((LANES, elems), 0)
    sub_hi = iota((groups, elems), 0)
    one_lo, one_hi = jnp.float32(1.0), jnp.float32(1.0)
    for a in range(basis):
        at = pl.ds(a * elems, elems)
        b_ref[:, at] = jnp.where(sub_lo == lo_ref[a : a + 1, :], one_lo, 0.0).astype(BF16)

    def corners(row_of, count):
        result = []
        for c in range(count):
            cols = []
            for h in range(halves):
                low = lo_ref[:, h * LANES : (h + 1) * LANES]
                high = hi_ref[:, h * LANES : (h + 1) * LANES]
                value = None
                for g in range(groups):
                    source = jnp.broadcast_to(row_of(c * groups + g), (ROWS, LANES))
                    got = pick(source, low)
                    value = got if value is None else jnp.where(high == g, got, value)
                cols.append(value)
            result.append(jnp.concatenate(cols, axis=1))
        return result

    def scatter(ys):
        for c in range(3):
            y_high = ys[c].astype(BF16).astype(F32)
            y_ref[c * ROWS : (c + 1) * ROWS, :] = y_high
            y_ref[(3 + c) * ROWS : (4 + c) * ROWS, :] = ys[c] - y_high
        for a in range(basis):
            at = pl.ds(a * elems, elems)
            chosen = jnp.where(alive, hi_ref[a : a + 1, :], groups) == sub_hi
            for i in range(6):
                z_ref[i * groups : (i + 1) * groups, at] = jnp.where(
                    chosen, y_ref[i * ROWS + a : i * ROWS + a + 1, :], 0.0
                ).astype(BF16)
        both = mm_nt(z_ref[...], b_ref[...])
        return both[0 : 3 * groups] + both[3 * groups :]

    s_low = jnp.broadcast_to(sent_nodes & (LANES - 1), (8, LANES))
    s_high = jnp.broadcast_to(sent_nodes >> 7, (8, LANES))

    def at_sent(sums):
        for c in range(3):
            for g in range(groups):
                r = c * groups + g
                s_ref[g * 8 + c : g * 8 + c + 1, :] = sums[r : r + 1, :]
        picked = jnp.zeros((8, LANES), F32)
        for g in range(groups):
            picked = jnp.where(s_high == g, pick(s_ref[g * 8 : g * 8 + 8, :], s_low), picked)
        return jnp.where(row < 3, picked, 0.0)

    def smoothed(near):
        return [mm3(smooth_parts, near[c]) for c in range(3)]

    def send_sums(sweep, value):
        v_send[sweep] = value
        for k in range(4):
            node_copy(sweep, k).start()

    sums = scatter(smoothed(corners(lambda r: x0_ref[r : r + 1, :], 3)))
    first_sent = at_sent(sums)
    pl.semaphore_wait(barrier, len(greeted))
    send_sums(0, first_sent)

    for v in range(fields):
        for h in range(halves):
            u_ref[0, v * ROWS : v * ROWS + basis, h * LANES : (h + 1) * LANES] = states[
                v * basis : (v + 1) * basis, h, :
            ]
    sent_elems = jnp.broadcast_to(flat(idx_ref[16:24, :], ghosts, 4), (8, LANES))
    sent_tile = [sent_elems]
    for t in range(1, tiles):
        sent_tile.append(pltpu.roll(sent_elems, ghosts * t, 1))
    first_of = [((slot_of + (slots - t)) & (slots - 1)) < 4 for t in range(tiles)]

    def choose(level, t, low, far):
        result = None
        for v in range(2 * t, min(2 * t + 2, fields)):
            got = None
            for h in range(halves):
                one = pick(u_ref[level, v * ROWS : (v + 1) * ROWS, h * LANES : (h + 1) * LANES], low)
                got = one if got is None else jnp.where(far == h, one, got)
            result = got if result is None else jnp.where(first_of[t], result, got)
        return result

    def send_ghosts(step):
        for k in range(4):
            tile = st_ref[step, 0]
            for t in range(1, tiles):
                tile = jnp.where(((slot_of + (slots - k)) & 3) == t, st_ref[step, t], tile)
            g_send[step, k] = tile
        for k in range(4):
            ghost_copy(step, k).start()

    for t in range(tiles):
        which = jnp.broadcast_to(sent_tile[t][0:1, :], (ROWS, LANES))
        st_ref[0, t] = choose(0, t, which & (LANES - 1), which >> 7)
    send_ghosts(0)

    got_lo, got_hi = got_nodes & (LANES - 1), got_nodes >> 7
    rb_ref[...] = jnp.where(iota((LANES, LANES), 0) == got_lo, one_lo, 0.0).astype(BF16)
    got_mask = iota((groups, LANES), 0) == got_hi
    for a in range(basis):
        at = pl.ds(a * elems, elems)
        z_ref[0:groups, at] = jnp.where(
            jnp.where(alive, hi_ref[a : a + 1, :], groups) == sub_hi, one_hi, 0.0
        ).astype(BF16)
    count = mm_nt(z_ref[0:groups, :], b_ref[...])
    count = count + mm_nt(jnp.where(got_mask, one_hi, 0.0).astype(BF16), rb_ref[...])
    half_inv = 0.5 / jnp.maximum(count, 1.0)
    hi_at_got = jnp.zeros((8, LANES), F32)
    got_lo8 = jnp.broadcast_to(got_lo, (8, LANES))
    got_hi8 = jnp.broadcast_to(got_hi, (8, LANES))
    for g in range(groups):
        hi_at_got = jnp.where(
            got_hi8 == g, pick(jnp.broadcast_to(half_inv[g : g + 1, :], (8, LANES)), got_lo8), hi_at_got
        )
    half_inv = jnp.concatenate([half_inv] * 3, axis=0)

    x_ref[...] = 0.5 * x0_ref[...] + sums * half_inv
    ahead = scatter(smoothed(corners(lambda r: x_ref[r : r + 1, :], 3)))
    ahead_sent = at_sent(ahead)

    square = (LANES, LANES)
    got_row = jnp.broadcast_to(got_nodes, square)
    got_col = jnp.transpose(got_row)
    sent_col = jnp.transpose(jnp.broadcast_to(sent_nodes, square))
    same = jnp.where(got_row == got_col, one_lo, 0.0).astype(BF16)
    marked = jnp.where((got_col & (LANES - 1)) == iota(square, 1), iota(square, 0) + 1, 0)
    col_hi = got_col >> 7
    table = [
        jnp.max(jnp.where(col_hi == g, marked, 0), axis=0, keepdims=True) for g in range(groups)
    ]
    sl_ref[...] = corners(lambda r: table[r], 1)[0]
    sent_wide = jnp.concatenate([sent_col] * halves, axis=1)
    for a in range(basis):
        node = jnp.where(alive, (hi_ref[a : a + 1, :] << 7) + lo_ref[a : a + 1, :], -1)
        gs_ref[:, pl.ds(a * elems, elems)] = jnp.where(sent_wide == node, one_lo, 0.0).astype(BF16)

    def gathered(sweep):
        for k in range(4):
            node_copy(sweep, k).wait_recv()
        arrived = v_recv[sweep, 0]
        for k in range(1, 4):
            arrived = jnp.where(lane // shared == k, v_recv[sweep, k], arrived)
        high, low = split(arrived)
        spread = (mm(high, same) + mm(low, same)) * hi_at_got
        near = []
        for c in range(3):
            cols = []
            for h in range(halves):
                index = sl_ref[:, h * LANES : (h + 1) * LANES]
                source = jnp.broadcast_to(spread[c : c + 1, :], (ROWS, LANES))
                cols.append(jnp.where(index > 0, pick(source, (index + (LANES - 1)) & (LANES - 1)), 0.0))
            near.append(jnp.concatenate(cols, axis=1))
        return arrived, near

    def to_sent(ys):
        for c in range(3):
            yr_ref[c] = ys[c]
        for a in range(basis):
            high, low = split(yr_ref[:, a, :])
            yw_ref[:, pl.ds(a * elems, elems)] = jnp.concatenate([high, low], axis=0)
        both = mm_nt(yw_ref[...], gs_ref[...])
        return both[0:8] + both[8:16]

    def injected(arrived):
        arr_high = arrived.astype(BF16).astype(F32)
        arr_low = arrived - arr_high
        pieces = [
            jnp.where(got_mask, part[c : c + 1, :], 0.0).astype(BF16)
            for part in (arr_high, arr_low) for c in range(3)
        ]
        both = mm_nt(jnp.concatenate(pieces, axis=0), rb_ref[...])
        return (both[0 : 3 * groups] + both[3 * groups :]) * half_inv

    def prepare_weights():
        for i in range(faces + 1):
            matrix = stiff[...] if i == 0 else lift[i - 1]
            pad_ref[i * ROWS : i * ROWS + basis, 0:basis] = jnp.dot(
                mass_inv[...], matrix, precision=HIGHEST, preferred_element_type=F32
            )
        wide = []
        for first in range(0, faces + 1, 4):
            total = None
            for i in range(first, min(first + 4, faces + 1)):
                block = pad_ref[i * ROWS : (i + 1) * ROWS, :]
                if i > first:
                    block = pltpu.roll(block, ROWS * (i - first), 1)
                total = block if total is None else total + block
            wide.append(total)
        w_high, w_low = split(jnp.concatenate(wide, axis=1))
        w_ref[0:ROWS, :] = w_high
        w_ref[ROWS : 2 * ROWS, :] = w_low
        for c in range(3):
            fg_ref[0:faces, c * ROWS : c * ROWS + basis] = face_geo[:, c, :]

    def gather_local(step):
        for v in range(fields):
            for h in range(halves):
                for f in range(faces):
                    which = jnp.broadcast_to(neighbours[f, h : h + 1, :], (ROWS, LANES))
                    low, far = which & (LANES - 1), which >> 7
                    got = None
                    for s in range(halves):
                        other = pick(u_ref[step, v * ROWS : (v + 1) * ROWS, s * LANES : (s + 1) * LANES], low)
                        got = other if got is None else jnp.where(far == s, other, got)
                    r = (v * faces + f) * ROWS
                    nb_ref[r : r + ROWS, h * LANES : (h + 1) * LANES] = got

    def gather_sent(step):
        for t in range(tiles):
            for f in range(faces):
                which = jnp.broadcast_to(nbs_ref[t, f : f + 1, :], (ROWS, LANES))
                nl_ref[t, f] = choose(step, t, which & (LANES - 1), which >> 7)

    def wait_ghosts(step):
        for k in range(4):
            ghost_copy(step, k).wait_recv()
        for t in range(tiles):
            tile = g_recv[step, 0]
            for k in range(1, 4):
                tile = jnp.where(((slot_of + (slots - t)) & 3) == k, g_recv[step, k], tile)
            gt_ref[t] = tile

    depth = (faces + 1) * ROWS

    def times(stack):
        high, low = split(jnp.concatenate(stack, axis=0))
        first = mm(w_ref[:, 0:depth], high)
        return first[0:ROWS] + (first[ROWS:] + mm(w_ref[0:ROWS, 0:depth], low))

    def advance_sent(step):
        stack = [jnp.concatenate([st_ref[step, t] for t in range(tiles)], axis=1)]
        for f in range(faces):
            cols = []
            for t in range(tiles):
                which = jnp.broadcast_to(nbs_ref[t, f : f + 1, :], (ROWS, LANES))
                at = which + jnp.where(first_of[t], ghosts * t, ghosts * (t + 4))
                got = jnp.where(which >= elems, pick(gt_ref[t], at & (LANES - 1)), nl_ref[t, f])
                cols.append(rs_ref[t, f : f + 1, :] * (got - st_ref[step, t]))
            stack.append(jnp.concatenate(cols, axis=1))
        new = times(stack)
        for t in range(tiles):
            kept = jnp.where(sent_tile[t][0:1, :] < live[0], 1.0, 0.0)
            st_ref[step + 1, t] = new[:, t * LANES : (t + 1) * LANES] * kept

    def change_of(v, step):
        u = u_ref[step, v * ROWS : (v + 1) * ROWS, :]
        stack = [u]
        for f in range(faces):
            cols = []
            r = (v * faces + f) * ROWS
            for h in range(halves):
                which = jnp.broadcast_to(neighbours[f, h : h + 1, :], (ROWS, LANES))
                got = pick(gt_ref[v // 2], (which + ghosts * (v // 2 + 4 * (v % 2))) & (LANES - 1))
                cols.append(jnp.where(which >= elems, got, nb_ref[r : r + ROWS, h * LANES : (h + 1) * LANES]))
            stack.append(rate_ref[f : f + 1, :] * (jnp.concatenate(cols, axis=1) - u))
        return times(stack)

    def finish_round(r, most):
        at = sum(len(p) for p in partners[:r])
        tile = m_send[r]
        for j in range(len(partners[r])):
            most_copy(r, j).wait_recv()
            tile = jnp.maximum(tile, m_recv[at + j])
        most = tile[0:1, 0:1]
        if r + 1 < len(partners):
            m_send[r + 1] = jnp.broadcast_to(most, (1, LANES))
            for j in range(len(partners[r + 1])):
                most_copy(r + 1, j).start()
        return most

    for sweep in range(SWEEPS - 1):
        arrived, near = gathered(sweep)
        ys = smoothed(near)
        send_sums(sweep + 1, ahead_sent + to_sent(ys))
        x_ref[...] = x_ref[...] + injected(arrived)
        sums = ahead + scatter(ys)
        x_ref[...] = 0.5 * x_ref[...] + sums * half_inv
        if sweep < SWEEPS - 2:
            ahead = scatter(smoothed(corners(lambda r: x_ref[r : r + 1, :], 3)))
            ahead_sent = at_sent(ahead)
            prepare_weights()

    geo_parts = split(fg_ref[:, 0 : 3 * ROWS])
    mv_ref[...] = x_ref[...] - x0_ref[...]
    projected = mm3(geo_parts, jnp.concatenate(corners(lambda r: mv_ref[r : r + 1, :], 3), axis=0))
    base = jnp.concatenate([rates[:, h, :] for h in range(halves)], axis=1)
    keep = jnp.where(alive, 1.0, 0.0)
    for t in range(tiles):
        low, far = sent_tile[t] & (LANES - 1), sent_tile[t] >> 7
        got = jnp.zeros((8, LANES), jnp.int32)
        for h in range(halves):
            nbp_ref[0:faces, :] = neighbours[:, h, :]
            got = jnp.where(far == h, pick(nbp_ref[...], low), got)
        nbs_ref[t] = got
    gather_sent(0)
    gather_local(0)
    wait_ghosts(0)

    arrived, near = gathered(SWEEPS - 1)
    projected = projected + mm3(geo_parts, jnp.concatenate(near, axis=0))
    rate = base * (1.0 + 0.5 * jnp.tanh(projected[0:faces])) * keep
    rate_ref[0:faces, :] = rate
    for t in range(tiles):
        low, far = sent_tile[t] & (LANES - 1), sent_tile[t] >> 7
        got = jnp.zeros((8, LANES), F32)
        for h in range(halves):
            got = jnp.where(far == h, pick(rate_ref[:, h * LANES : (h + 1) * LANES], low), got)
        rs_ref[t] = got
    advance_sent(0)
    send_ghosts(1)
    most = jnp.max(jnp.sum(rate, axis=0, keepdims=True), axis=1, keepdims=True)
    m_send[0] = jnp.broadcast_to(most, (1, LANES))
    for j in range(len(partners[0]) if rounds else 0):
        most_copy(0, j).start()
    out_c[...] = x_ref[...] + injected(arrived)

    for step in range(STEPS - 1):
        for v in range(fields):
            u_ref[step + 1, v * ROWS : (v + 1) * ROWS, :] = keep * change_of(v, step)
        if step + 2 < STEPS:
            gather_sent(step + 1)
        gather_local(step + 1)
        if step == STEPS - 2:
            for r in range(step, len(partners)):
                most = finish_round(r, most)
            scale = jnp.broadcast_to(CFL / most, (ROWS, elems))
            for v in range(fields):
                total = math.comb(STEPS, STEPS - 1) * u_ref[STEPS - 1, v * ROWS : (v + 1) * ROWS, :]
                for k in range(STEPS - 2, -1, -1):
                    total = math.comb(STEPS, k) * u_ref[k, v * ROWS : (v + 1) * ROWS, :] + scale * total
                u_ref[STEPS, v * ROWS : (v + 1) * ROWS, :] = total
        wait_ghosts(step + 1)
        if step + 2 < STEPS:
            advance_sent(step + 1)
            send_ghosts(step + 2)
        if step < min(STEPS - 2, len(partners)):
            most = finish_round(step, most)
    scale = keep * (scale * scale) * (scale * scale)
    for v in range(fields):
        new = u_ref[STEPS, v * ROWS : (v + 1) * ROWS, :] + scale * change_of(v, STEPS - 1)
        for h in range(halves):
            out_u[v * basis : (v + 1) * basis, h, :] = new[0:basis, h * LANES : (h + 1) * LANES]

    for sweep in range(SWEEPS):
        for k in range(4):
            node_copy(sweep, k).wait_send()
    for step in range(STEPS):
        for k in range(4):
            ghost_copy(step, k).wait_send()
    for r, one in enumerate(partners):
        for j in range(len(one)):
            most_copy(r, j).wait_send()


def hand_over(coords, remapped, out_c, out_u, held_c, held_u, sem):
    half = remapped.shape[0] // 2
    parts = [(coords, held_c, out_c)]
    for at in (pl.ds(0, half), pl.ds(half, remapped.shape[0] - half)):
        parts.append((remapped.at[at], held_u.at[at], out_u.at[at]))
    reads = [pltpu.make_async_copy(a, b, sem.at[0, i]) for i, (a, b, _) in enumerate(parts)]
    writes = [pltpu.make_async_copy(b, c, sem.at[1, i]) for i, (_, b, c) in enumerate(parts)]
    for one in reads:
        one.start()
    for read, write in zip(reads, writes):
        read.wait()
        write.start()
    for one in writes:
        one.wait()


def on_device(*args):
    pos, states, conn = args[:3]
    parts = lax.axis_size("dom")
    w = max(parts // 8, 1)
    shifts = (1, -1, w, -w)
    rounds = rounds_of(parts)
    total = sum(r - 1 for r, _ in rounds)
    basis, elems = conn.shape[1:]
    fields, faces = states.shape[1], args[6].shape[1]
    groups = pos.shape[2] // LANES
    nodes = pos.shape[2]
    halves = elems // LANES
    tiles = (fields + 1) // 2
    flat = list(args)
    for i, rows in ((0, 3 * groups), (1, fields * basis * halves), (2, basis * halves), (6, faces * halves), (10, faces * halves)):
        flat[i] = args[i].reshape(rows, LANES) if i == 0 else args[i].reshape(rows // halves, halves, LANES)
    for i in (3, 4, 5):
        flat[i] = args[i][0]
    vmem = pl.BlockSpec(memory_space=pltpu.VMEM)
    smem = pl.BlockSpec(memory_space=pltpu.SMEM)
    hbm = pl.BlockSpec(memory_space=pl.ANY)
    specs = [smem if i == 7 else hbm for i in range(len(args))]
    held = [pltpu.VMEM(a.shape, a.dtype) for i, a in enumerate(flat) if i != 7]
    scratch = held + [
        pltpu.SemaphoreType.DMA((len(held),)),
        pltpu.VMEM((3 * groups, LANES), F32),
        pltpu.VMEM((8 * groups, LANES), F32),
        pltpu.VMEM((ROWS, elems), jnp.int32),
        pltpu.VMEM((ROWS, elems), jnp.int32),
        pltpu.VMEM((6 * ROWS, elems), F32),
        pltpu.VMEM((6 * groups, basis * elems), BF16),
        pltpu.VMEM((LANES, basis * elems), BF16),
        pltpu.VMEM((LANES, LANES), BF16),
        pltpu.VMEM((STEPS + 1, fields * ROWS, elems), F32),
        pltpu.VMEM((fields * faces * ROWS, elems), F32),
        pltpu.VMEM((8, elems), F32),
        pltpu.VMEM(((faces + 1) * ROWS, LANES), F32),
        pltpu.VMEM((8, LANES), F32),
        pltpu.VMEM((2 * ROWS, 2 * LANES), BF16),
        pltpu.VMEM((24, LANES), jnp.int32),
        pltpu.VMEM((3 * groups, LANES), F32),
        pltpu.VMEM((8, ROWS, elems), F32),
        pltpu.VMEM((16, basis * elems), BF16),
        pltpu.VMEM((LANES, basis * elems), BF16),
        pltpu.VMEM((ROWS, elems), jnp.int32),
        pltpu.VMEM((STEPS, tiles, ROWS, LANES), F32),
        pltpu.VMEM((tiles, ROWS, LANES), F32),
        pltpu.VMEM((tiles, faces, ROWS, LANES), F32),
        pltpu.VMEM((tiles, 8, LANES), jnp.int32),
        pltpu.VMEM((tiles, 8, LANES), F32),
        pltpu.VMEM((8, LANES), jnp.int32),
        pltpu.VMEM((SWEEPS, 8, LANES), F32),
        pltpu.VMEM((SWEEPS, 4, 8, LANES), F32),
        pltpu.VMEM((STEPS, 4, ROWS, LANES), F32),
        pltpu.VMEM((STEPS, 4, ROWS, LANES), F32),
        pltpu.VMEM((max(len(rounds), 1), 1, LANES), F32),
        pltpu.VMEM((max(total, 1), 1, LANES), F32),
        pltpu.SemaphoreType.DMA((SWEEPS, 4)),
        pltpu.SemaphoreType.DMA((SWEEPS, 4)),
        pltpu.SemaphoreType.DMA((STEPS, 4)),
        pltpu.SemaphoreType.DMA((STEPS, 4)),
        pltpu.SemaphoreType.DMA((max(total, 1),)),
        pltpu.SemaphoreType.DMA((max(total, 1),)),
    ]
    coords, remapped = pl.pallas_call(
        functools.partial(kernel, parts, shifts, rounds, basis, elems, fields, faces, nodes),
        out_shape=(
            jax.ShapeDtypeStruct((3 * groups, LANES), F32),
            jax.ShapeDtypeStruct((fields * basis, halves, LANES), F32),
        ),
        in_specs=specs,
        out_specs=(vmem, vmem),
        scratch_shapes=scratch,
        compiler_params=pltpu.CompilerParams(
            collective_id=0, has_side_effects=True, vmem_limit_bytes=60 * 1024 * 1024
        ),
    )(*flat)
    coords, remapped = pl.pallas_call(
        hand_over,
        out_shape=(
            jax.ShapeDtypeStruct(coords.shape, F32),
            jax.ShapeDtypeStruct(remapped.shape, F32),
        ),
        in_specs=[hbm, hbm],
        out_specs=(hbm, hbm),
        scratch_shapes=[
            pltpu.VMEM(coords.shape, F32),
            pltpu.VMEM(remapped.shape, F32),
            pltpu.SemaphoreType.DMA((2, 3)),
        ],
        compiler_params=pltpu.CompilerParams(vmem_limit_bytes=60 * 1024 * 1024),
    )(coords, remapped)
    return coords.reshape(pos.shape), remapped.reshape(states.shape)


def solution(mesh):
    dom = lambda rank: P("dom", *([None] * (rank - 1)))
    in_specs = (
        dom(3), dom(4), dom(3), dom(3), dom(3), dom(3), dom(3), P("dom"),
        P(), P(), dom(3), P(), P(), P(),
    )
    return jax.shard_map(
        on_device, mesh=mesh, in_specs=in_specs, out_specs=(dom(3), dom(4)), check_vma=False
    )
```

```python
import functools
import math

import jax
import jax.numpy as jnp
from jax import lax
from jax.experimental import pallas as pl
from jax.experimental.pallas import tpu as pltpu
from jax.sharding import PartitionSpec as P

SWEEPS = 3
STEPS = 4
CFL = 0.4
F32 = jnp.float32
BF16 = jnp.bfloat16
HIGHEST = lax.Precision.HIGHEST
MESH = pl.DeviceIdType.MESH
LANES = 128
ROWS = 32
RADIX = 8


def rounds_of(parts):
    found, stride = [], 1
    while parts > 1:
        radix = max(r for r in range(1, RADIX + 1) if parts % r == 0)
        if radix == 1:
            radix = parts
        found.append((radix, stride))
        stride *= radix
        parts //= radix
    return found


def pick(table, index):
    return jnp.take_along_axis(table, index, axis=1, mode="promise_in_bounds")


def split(x):
    high = x.astype(BF16)
    low = (x - high.astype(F32)).astype(BF16)
    return high, low


def mm(a, b):
    return jnp.dot(a, b, preferred_element_type=F32)


def mm3(a, b):
    high, low = split(b)
    return mm(a[0], high) + (mm(a[1], high) + mm(a[0], low))


def mm_nt(a, b):
    return lax.dot_general(a, b, (((1,), (1,)), ((), ())), preferred_element_type=F32)


def iota(shape, dim):
    return lax.broadcasted_iota(jnp.int32, shape, dim)


def kernel(
    parts, shifts, rounds,
    basis, elems, fields, faces, nodes,
    pos_any, states_any, conn_any, send_nodes_any, recv_nodes_any, send_elems_any, neighbours_any, live,
    smooth_any, face_geo_any, rates_any, stiff_any, lift_any, mass_inv_any,
    out_c, out_u,
    x0_ref, states, conn, send_nodes, recv_nodes, send_elems, neighbours,
    smooth, face_geo, rates, stiff, lift, mass_inv, sent_smem, in_sem,
    x_ref, s_ref, lo_ref, hi_ref, y_ref, z_ref, b_ref, rb_ref,
    u_ref, nb_ref, rate_ref, pad_ref, fg_ref, w_ref, idx_ref,
    mv_ref, cm_ref, ka_ref, kb_ref, oh_ref, hs_ref, gr_ref, tt_ref, sl_ref, st_ref, gt_ref, nl_ref, nbs_ref, rs_ref, nbp_ref,
    v_send, v_recv, g_send, g_recv, m_send, m_recv,
    vs_sem, vr_sem, gs_sem, gr_sem, ms_sem, mr_sem,
):
    me = lax.axis_index("dom")
    groups = nodes // LANES
    halves = elems // LANES
    shared = send_nodes.shape[1]
    ghosts = send_elems.shape[1]
    slots = LANES // ghosts

    sources = (
        conn_any, pos_any, states_any, send_elems_any, send_nodes_any, recv_nodes_any, smooth_any,
        neighbours_any, rates_any, face_geo_any, mass_inv_any, stiff_any, lift_any, send_nodes_any,
    )
    places = (
        conn, x0_ref, states, send_elems, send_nodes, recv_nodes, smooth,
        neighbours, rates, face_geo, mass_inv, stiff, lift, sent_smem,
    )
    loads = [
        pltpu.make_async_copy(a, b, in_sem.at[i]) for i, (a, b) in enumerate(zip(sources, places))
    ]
    for one in loads:
        one.start()

    partners = []
    for radix, stride in rounds:
        digit = lax.rem(me // stride, radix)
        partners.append(
            [me + (lax.rem(digit + j, radix) - digit) * stride for j in range(1, radix)]
        )
    targets = [lax.rem(me + o + parts, parts) for o in shifts]

    barrier = pltpu.get_barrier_semaphore()
    greeted = targets + [t for one in partners for t in one]
    for t in greeted:
        pl.semaphore_signal(barrier, inc=1, device_id=(t,), device_id_type=MESH)

    def node_copy(sweep, k):
        return pltpu.make_async_remote_copy(
            src_ref=v_send.at[sweep], dst_ref=v_recv.at[sweep, k],
            send_sem=vs_sem.at[sweep, k], recv_sem=vr_sem.at[sweep, k],
            device_id=(targets[k],), device_id_type=MESH,
        )

    def ghost_copy(step, k):
        return pltpu.make_async_remote_copy(
            src_ref=g_send.at[step, k], dst_ref=g_recv.at[step, k],
            send_sem=gs_sem.at[step, k], recv_sem=gr_sem.at[step, k],
            device_id=(targets[k],), device_id_type=MESH,
        )

    def most_copy(r, j):
        at = sum(len(p) for p in partners[:r]) + j
        return pltpu.make_async_remote_copy(
            src_ref=m_send.at[r], dst_ref=m_recv.at[at],
            send_sem=ms_sem.at[at], recv_sem=mr_sem.at[at],
            device_id=(partners[r][j],), device_id_type=MESH,
        )

    lane = iota((8, LANES), 1)
    row = iota((8, LANES), 0)
    slot_of = iota((ROWS, LANES), 1) // ghosts
    tiles = (fields + 1) // 2

    idx_ref[...] = jnp.zeros(idx_ref.shape, jnp.int32)
    lo_ref[...] = jnp.zeros(lo_ref.shape, jnp.int32)
    hi_ref[...] = jnp.zeros(hi_ref.shape, jnp.int32)
    s_ref[...] = jnp.zeros(s_ref.shape, F32)
    u_ref[0] = jnp.zeros(u_ref.shape[1:], F32)
    cm_ref[...] = jnp.full(cm_ref.shape, -1, jnp.int32)
    ka_ref[...] = jnp.zeros(ka_ref.shape, F32)
    kb_ref[...] = jnp.zeros(kb_ref.shape, F32)
    pad_ref[...] = jnp.zeros(pad_ref.shape, F32)
    fg_ref[...] = jnp.zeros(fg_ref.shape, F32)
    nbp_ref[...] = jnp.zeros(nbp_ref.shape, jnp.int32)
    rate_ref[...] = jnp.zeros(rate_ref.shape, F32)
    alive = iota((1, elems), 1) < live[0]
    for one in loads:
        one.wait()

    pad_ref[0:basis, 0:basis] = smooth[...]
    smooth_parts = split(pad_ref[0:ROWS, 0:ROWS])
    idx_ref[0:4, 0:shared] = send_nodes[...]
    idx_ref[8:12, 0:shared] = recv_nodes[...]
    idx_ref[16:20, 0:ghosts] = send_elems[...]

    def flat(block, width, count):
        spread = pick(block, lax.rem(lane, width))
        kept = jnp.where(lax.rem(lane // width, count) == row, spread, 0)
        return jnp.sum(kept, axis=0, keepdims=True)

    sent_nodes = flat(idx_ref[0:8, :], shared, 4)
    got_nodes = flat(idx_ref[8:16, :], shared, 4)

    for h in range(halves):
        part = conn[:, h, :]
        lo_ref[0:basis, h * LANES : (h + 1) * LANES] = part & (LANES - 1)
        hi_ref[0:basis, h * LANES : (h + 1) * LANES] = part >> 7
        cm_ref[0:basis, h * LANES : (h + 1) * LANES] = part
    cm_ref[...] = jnp.where(alive, cm_ref[...], -1)

    sub_lo = iota((LANES, elems), 0)
    sub_hi = iota((groups, elems), 0)
    one_lo, one_hi = jnp.float32(1.0), jnp.float32(1.0)
    for a in range(basis):
        at = pl.ds(a * elems, elems)
        b_ref[:, at] = jnp.where(sub_lo == lo_ref[a : a + 1, :], one_lo, 0.0).astype(BF16)

    def corners(row_of, count):
        result = []
        for c in range(count):
            cols = []
            for h in range(halves):
                low = lo_ref[:, h * LANES : (h + 1) * LANES]
                high = hi_ref[:, h * LANES : (h + 1) * LANES]
                value = None
                for g in range(groups):
                    source = jnp.broadcast_to(row_of(c * groups + g), (ROWS, LANES))
                    got = pick(source, low)
                    value = got if value is None else jnp.where(high == g, got, value)
                cols.append(value)
            result.append(jnp.concatenate(cols, axis=1))
        return result

    def scatter(ys, counting=False):
        for c in range(3):
            y_high = ys[c].astype(BF16).astype(F32)
            y_ref[c * ROWS : (c + 1) * ROWS, :] = y_high
            y_ref[(3 + c) * ROWS : (4 + c) * ROWS, :] = ys[c] - y_high
        for a in range(basis):
            at = pl.ds(a * elems, elems)
            chosen = jnp.where(alive, hi_ref[a : a + 1, :], groups) == sub_hi
            for i in range(6):
                z_ref[i * groups : (i + 1) * groups, at] = jnp.where(
                    chosen, y_ref[i * ROWS + a : i * ROWS + a + 1, :], 0.0
                ).astype(BF16)
            if counting:
                z_ref[6 * groups : 7 * groups, at] = jnp.where(chosen, one_hi, 0.0).astype(BF16)
        rows = (7 if counting else 6) * groups
        both = mm_nt(z_ref[0:rows, :], b_ref[...])
        result = both[0 : 3 * groups] + both[3 * groups : 6 * groups]
        return (result, both[6 * groups :]) if counting else result

    s_low = jnp.broadcast_to(sent_nodes & (LANES - 1), (8, LANES))
    s_high = jnp.broadcast_to(sent_nodes >> 7, (8, LANES))

    def at_sent(sums):
        for c in range(3):
            for g in range(groups):
                r = c * groups + g
                s_ref[g * 8 + c : g * 8 + c + 1, :] = sums[r : r + 1, :]
        picked = jnp.zeros((8, LANES), F32)
        for g in range(groups):
            picked = jnp.where(s_high == g, pick(s_ref[g * 8 : g * 8 + 8, :], s_low), picked)
        return jnp.where(row < 3, picked, 0.0)

    def smoothed(near):
        return [mm3(smooth_parts, near[c]) for c in range(3)]

    def send_sums(sweep, value):
        v_send[sweep] = value
        for k in range(4):
            node_copy(sweep, k).start()

    sums, count = scatter(smoothed(corners(lambda r: x0_ref[r : r + 1, :], 3)), True)
    first_sent = at_sent(sums)
    pl.semaphore_wait(barrier, len(greeted))
    send_sums(0, first_sent)

    sent_elems = jnp.broadcast_to(flat(idx_ref[16:24, :], ghosts, 4), (8, LANES))
    sent_tile = [sent_elems]
    for t in range(1, tiles):
        sent_tile.append(pltpu.roll(sent_elems, ghosts * t, 1))
    first_of = [((slot_of + (slots - t)) & (slots - 1)) < 4 for t in range(tiles)]

    def choose(level, t, low, far):
        result = None
        for v in range(2 * t, min(2 * t + 2, fields)):
            got = None
            for h in range(halves):
                one = pick(u_ref[level, v * ROWS : (v + 1) * ROWS, h * LANES : (h + 1) * LANES], low)
                got = one if got is None else jnp.where(far == h, one, got)
            result = got if result is None else jnp.where(first_of[t], result, got)
        return result

    def send_ghosts(step):
        for k in range(4):
            tile = st_ref[step, 0]
            for t in range(1, tiles):
                tile = jnp.where(((slot_of + (slots - k)) & 3) == t, st_ref[step, t], tile)
            g_send[step, k] = tile
        for k in range(4):
            ghost_copy(step, k).start()

    got_lo, got_hi = got_nodes & (LANES - 1), got_nodes >> 7
    rb_ref[...] = jnp.where(iota((LANES, LANES), 0) == got_lo, one_lo, 0.0).astype(BF16)
    got_mask = iota((groups, LANES), 0) == got_hi
    count = count + mm_nt(jnp.where(got_mask, one_hi, 0.0).astype(BF16), rb_ref[...])
    half_inv = 0.5 / jnp.maximum(count, 1.0)
    hi_at_got = jnp.zeros((8, LANES), F32)
    got_lo8 = jnp.broadcast_to(got_lo, (8, LANES))
    got_hi8 = jnp.broadcast_to(got_hi, (8, LANES))
    for g in range(groups):
        hi_at_got = jnp.where(
            got_hi8 == g, pick(jnp.broadcast_to(half_inv[g : g + 1, :], (8, LANES)), got_lo8), hi_at_got
        )
    half_inv = jnp.concatenate([half_inv] * 3, axis=0)

    x_ref[...] = 0.5 * x0_ref[...] + sums * half_inv
    ahead = scatter(smoothed(corners(lambda r: x_ref[r : r + 1, :], 3)))
    ahead_sent = at_sent(ahead)

    square = (LANES, LANES)
    got_row = jnp.broadcast_to(got_nodes, square)
    got_col = jnp.transpose(got_row)
    got_wide = jnp.concatenate([got_col] * halves, axis=1)
    for a in range(basis):
        node = cm_ref[a : a + 1, :]
        gr_ref[:, pl.ds(a * elems, elems)] = jnp.where(got_wide == node, one_lo, 0.0).astype(BF16)
    turned = jnp.transpose(pad_ref[0:LANES, :])[0:ROWS, :]
    for i in range(8):
        place = ka_ref if i < 4 else kb_ref
        placed = turned if i % 4 == 0 else pltpu.roll(turned, ROWS * (i % 4), 1)
        place[pl.ds(i, basis, stride=8), :] = placed[0:basis, :]
    k8_high, k8_low = split(jnp.concatenate([ka_ref[...], kb_ref[...]], axis=1))
    for pair in range(LANES // 16):
        both = []
        for part in range(2):
            for i in range(8):
                slot = pair * 16 + part * 8 + i
                node = sent_smem[slot // shared, slot % shared]
                oh_ref[part, i * ROWS : (i + 1) * ROWS, :] = jnp.where(
                    cm_ref[...] == node, one_lo, 0.0
                ).astype(BF16)
            both.append(mm(k8_high, oh_ref[part]) + mm(k8_low, oh_ref[part]))
        for b in range(basis):
            block = jnp.concatenate([one[b * 8 : (b + 1) * 8] for one in both], axis=0)
            high, low = split(block)
            at = pl.ds(b * elems, elems)
            hs_ref[pair * 16 : (pair + 1) * 16, at] = high
            hs_ref[LANES + pair * 16 : LANES + (pair + 1) * 16, at] = low
    response = mm_nt(hs_ref[...], gr_ref[...])
    response = split((response[0:LANES] + response[LANES:]) * hi_at_got[0:1, :])
    for i in range(2):
        tt_ref[i] = response[i]

    def to_sent(arrived):
        high, low = split(arrived)
        return mm_nt(high, tt_ref[0]) + (mm_nt(low, tt_ref[0]) + mm_nt(high, tt_ref[1]))

    def prepare_slots():
        marked = jnp.where((got_col & (LANES - 1)) == iota(square, 1), iota(square, 0) + 1, 0)
        col_hi = got_col >> 7
        table = [
            jnp.max(jnp.where(col_hi == g, marked, 0), axis=0, keepdims=True) for g in range(groups)
        ]
        sl_ref[...] = corners(lambda r: table[r], 1)[0]

    def received(sweep):
        for k in range(4):
            node_copy(sweep, k).wait_recv()
        arrived = v_recv[sweep, 0]
        for k in range(1, 4):
            arrived = jnp.where(lane // shared == k, v_recv[sweep, k], arrived)
        return arrived

    same = jnp.where(got_row == got_col, one_lo, 0.0).astype(BF16)

    def gathered(arrived):
        high, low = split(arrived)
        spread = (mm(high, same) + mm(low, same)) * hi_at_got
        near = []
        for c in range(3):
            cols = []
            for h in range(halves):
                index = sl_ref[:, h * LANES : (h + 1) * LANES]
                source = jnp.broadcast_to(spread[c : c + 1, :], (ROWS, LANES))
                cols.append(jnp.where(index > 0, pick(source, (index + (LANES - 1)) & (LANES - 1)), 0.0))
            near.append(jnp.concatenate(cols, axis=1))
        return near

    def injected(arrived):
        arr_high = arrived.astype(BF16).astype(F32)
        arr_low = arrived - arr_high
        pieces = [
            jnp.where(got_mask, part[c : c + 1, :], 0.0).astype(BF16)
            for part in (arr_high, arr_low) for c in range(3)
        ]
        both = mm_nt(jnp.concatenate(pieces, axis=0), rb_ref[...])
        return (both[0 : 3 * groups] + both[3 * groups :]) * half_inv

    def prepare_weights():
        for i in range(faces + 1):
            matrix = stiff[...] if i == 0 else lift[i - 1]
            pad_ref[i * ROWS : i * ROWS + basis, 0:basis] = jnp.dot(
                mass_inv[...], matrix, precision=HIGHEST, preferred_element_type=F32
            )
        wide = []
        for first in range(0, faces + 1, 4):
            total = None
            for i in range(first, min(first + 4, faces + 1)):
                block = pad_ref[i * ROWS : (i + 1) * ROWS, :]
                if i > first:
                    block = pltpu.roll(block, ROWS * (i - first), 1)
                total = block if total is None else total + block
            wide.append(total)
        w_high, w_low = split(jnp.concatenate(wide, axis=1))
        w_ref[0:ROWS, :] = w_high
        w_ref[ROWS : 2 * ROWS, :] = w_low
        for c in range(3):
            fg_ref[0:faces, c * ROWS : c * ROWS + basis] = face_geo[:, c, :]

    def gather_local(step):
        for v in range(fields):
            for h in range(halves):
                for f in range(faces):
                    which = jnp.broadcast_to(neighbours[f, h : h + 1, :], (ROWS, LANES))
                    low, far = which & (LANES - 1), which >> 7
                    got = None
                    for s in range(halves):
                        other = pick(u_ref[step, v * ROWS : (v + 1) * ROWS, s * LANES : (s + 1) * LANES], low)
                        got = other if got is None else jnp.where(far == s, other, got)
                    r = (v * faces + f) * ROWS
                    nb_ref[r : r + ROWS, h * LANES : (h + 1) * LANES] = got

    def gather_sent(step):
        for t in range(tiles):
            for f in range(faces):
                which = jnp.broadcast_to(nbs_ref[t, f : f + 1, :], (ROWS, LANES))
                nl_ref[t, f] = choose(step, t, which & (LANES - 1), which >> 7)

    def wait_ghosts(step):
        for k in range(4):
            ghost_copy(step, k).wait_recv()
        for t in range(tiles):
            tile = g_recv[step, 0]
            for k in range(1, 4):
                tile = jnp.where(((slot_of + (slots - t)) & 3) == k, g_recv[step, k], tile)
            gt_ref[t] = tile

    depth = (faces + 1) * ROWS

    def times(stack):
        high, low = split(jnp.concatenate(stack, axis=0))
        first = mm(w_ref[:, 0:depth], high)
        return first[0:ROWS] + (first[ROWS:] + mm(w_ref[0:ROWS, 0:depth], low))

    def advance_sent(step):
        stack = [jnp.concatenate([st_ref[step, t] for t in range(tiles)], axis=1)]
        for f in range(faces):
            cols = []
            for t in range(tiles):
                which = jnp.broadcast_to(nbs_ref[t, f : f + 1, :], (ROWS, LANES))
                at = which + jnp.where(first_of[t], ghosts * t, ghosts * (t + 4))
                got = jnp.where(which >= elems, pick(gt_ref[t], at & (LANES - 1)), nl_ref[t, f])
                cols.append(rs_ref[t, f : f + 1, :] * (got - st_ref[step, t]))
            stack.append(jnp.concatenate(cols, axis=1))
        new = times(stack)
        for t in range(tiles):
            kept = jnp.where(sent_tile[t][0:1, :] < live[0], 1.0, 0.0)
            st_ref[step + 1, t] = new[:, t * LANES : (t + 1) * LANES] * kept

    def change_of(v, step):
        u = u_ref[step, v * ROWS : (v + 1) * ROWS, :]
        stack = [u]
        for f in range(faces):
            cols = []
            r = (v * faces + f) * ROWS
            for h in range(halves):
                which = jnp.broadcast_to(neighbours[f, h : h + 1, :], (ROWS, LANES))
                got = pick(gt_ref[v // 2], (which + ghosts * (v // 2 + 4 * (v % 2))) & (LANES - 1))
                cols.append(jnp.where(which >= elems, got, nb_ref[r : r + ROWS, h * LANES : (h + 1) * LANES]))
            stack.append(rate_ref[f : f + 1, :] * (jnp.concatenate(cols, axis=1) - u))
        return times(stack)

    def finish_round(r, most):
        at = sum(len(p) for p in partners[:r])
        tile = m_send[r]
        for j in range(len(partners[r])):
            most_copy(r, j).wait_recv()
            tile = jnp.maximum(tile, m_recv[at + j])
        most = tile[0:1, 0:1]
        if r + 1 < len(partners):
            m_send[r + 1] = jnp.broadcast_to(most, (1, LANES))
            for j in range(len(partners[r + 1])):
                most_copy(r + 1, j).start()
        return most

    for sweep in range(SWEEPS - 1):
        arrived = received(sweep)
        send_sums(sweep + 1, ahead_sent + to_sent(arrived))
        if sweep == 0:
            for v in range(fields):
                for h in range(halves):
                    u_ref[0, v * ROWS : v * ROWS + basis, h * LANES : (h + 1) * LANES] = states[
                        v * basis : (v + 1) * basis, h, :
                    ]
            for t in range(tiles):
                which = jnp.broadcast_to(sent_tile[t][0:1, :], (ROWS, LANES))
                st_ref[0, t] = choose(0, t, which & (LANES - 1), which >> 7)
            send_ghosts(0)
            prepare_slots()
        ys = smoothed(gathered(arrived))
        x_ref[...] = x_ref[...] + injected(arrived)
        sums = ahead + scatter(ys)
        x_ref[...] = 0.5 * x_ref[...] + sums * half_inv
        if sweep < SWEEPS - 2:
            ahead = scatter(smoothed(corners(lambda r: x_ref[r : r + 1, :], 3)))
            ahead_sent = at_sent(ahead)

    prepare_weights()
    geo_parts = split(fg_ref[:, 0 : 3 * ROWS])
    mv_ref[...] = x_ref[...] - x0_ref[...]
    projected = mm3(geo_parts, jnp.concatenate(corners(lambda r: mv_ref[r : r + 1, :], 3), axis=0))
    base = jnp.concatenate([rates[:, h, :] for h in range(halves)], axis=1)
    keep = jnp.where(alive, 1.0, 0.0)
    for t in range(tiles):
        low, far = sent_tile[t] & (LANES - 1), sent_tile[t] >> 7
        got = jnp.zeros((8, LANES), jnp.int32)
        for h in range(halves):
            nbp_ref[0:faces, :] = neighbours[:, h, :]
            got = jnp.where(far == h, pick(nbp_ref[...], low), got)
        nbs_ref[t] = got
    gather_sent(0)
    gather_local(0)
    wait_ghosts(0)

    arrived = received(SWEEPS - 1)
    near = gathered(arrived)
    projected = projected + mm3(geo_parts, jnp.concatenate(near, axis=0))
    rate = base * (1.0 + 0.5 * jnp.tanh(projected[0:faces])) * keep
    rate_ref[0:faces, :] = rate
    for t in range(tiles):
        low, far = sent_tile[t] & (LANES - 1), sent_tile[t] >> 7
        got = jnp.zeros((8, LANES), F32)
        for h in range(halves):
            got = jnp.where(far == h, pick(rate_ref[:, h * LANES : (h + 1) * LANES], low), got)
        rs_ref[t] = got
    advance_sent(0)
    send_ghosts(1)
    most = jnp.max(jnp.sum(rate, axis=0, keepdims=True), axis=1, keepdims=True)
    m_send[0] = jnp.broadcast_to(most, (1, LANES))
    for j in range(len(partners[0]) if rounds else 0):
        most_copy(0, j).start()
    out_c[...] = x_ref[...] + injected(arrived)

    for step in range(STEPS - 1):
        for v in range(fields):
            u_ref[step + 1, v * ROWS : (v + 1) * ROWS, :] = keep * change_of(v, step)
        if step + 2 < STEPS:
            gather_sent(step + 1)
        gather_local(step + 1)
        if step == STEPS - 2:
            for r in range(step, len(partners)):
                most = finish_round(r, most)
            scale = jnp.broadcast_to(CFL / most, (ROWS, elems))
            for v in range(fields):
                total = math.comb(STEPS, STEPS - 1) * u_ref[STEPS - 1, v * ROWS : (v + 1) * ROWS, :]
                for k in range(STEPS - 2, -1, -1):
                    total = math.comb(STEPS, k) * u_ref[k, v * ROWS : (v + 1) * ROWS, :] + scale * total
                u_ref[STEPS, v * ROWS : (v + 1) * ROWS, :] = total
        wait_ghosts(step + 1)
        if step + 2 < STEPS:
            advance_sent(step + 1)
            send_ghosts(step + 2)
        if step < min(STEPS - 2, len(partners)):
            most = finish_round(step, most)
    scale = keep * (scale * scale) * (scale * scale)
    for v in range(fields):
        new = u_ref[STEPS, v * ROWS : (v + 1) * ROWS, :] + scale * change_of(v, STEPS - 1)
        for h in range(halves):
            out_u[v * basis : (v + 1) * basis, h, :] = new[0:basis, h * LANES : (h + 1) * LANES]

    for sweep in range(SWEEPS):
        for k in range(4):
            node_copy(sweep, k).wait_send()
    for step in range(STEPS):
        for k in range(4):
            ghost_copy(step, k).wait_send()
    for r, one in enumerate(partners):
        for j in range(len(one)):
            most_copy(r, j).wait_send()


def hand_over(coords, remapped, out_c, out_u, held_c, held_u, sem):
    half = remapped.shape[0] // 2
    parts = [(coords, held_c, out_c)]
    for at in (pl.ds(0, half), pl.ds(half, remapped.shape[0] - half)):
        parts.append((remapped.at[at], held_u.at[at], out_u.at[at]))
    reads = [pltpu.make_async_copy(a, b, sem.at[0, i]) for i, (a, b, _) in enumerate(parts)]
    writes = [pltpu.make_async_copy(b, c, sem.at[1, i]) for i, (_, b, c) in enumerate(parts)]
    for one in reads:
        one.start()
    for read, write in zip(reads, writes):
        read.wait()
        write.start()
    for one in writes:
        one.wait()


def on_device(*args):
    pos, states, conn = args[:3]
    parts = lax.axis_size("dom")
    w = max(parts // 8, 1)
    shifts = (1, -1, w, -w)
    rounds = rounds_of(parts)
    total = sum(r - 1 for r, _ in rounds)
    basis, elems = conn.shape[1:]
    fields, faces = states.shape[1], args[6].shape[1]
    groups = pos.shape[2] // LANES
    nodes = pos.shape[2]
    halves = elems // LANES
    tiles = (fields + 1) // 2
    flat = list(args)
    for i, rows in ((0, 3 * groups), (1, fields * basis * halves), (2, basis * halves), (6, faces * halves), (10, faces * halves)):
        flat[i] = args[i].reshape(rows, LANES) if i == 0 else args[i].reshape(rows // halves, halves, LANES)
    for i in (3, 4, 5):
        flat[i] = args[i][0]
    vmem = pl.BlockSpec(memory_space=pltpu.VMEM)
    smem = pl.BlockSpec(memory_space=pltpu.SMEM)
    hbm = pl.BlockSpec(memory_space=pl.ANY)
    specs = [smem if i == 7 else hbm for i in range(len(args))]
    held = [pltpu.VMEM(a.shape, a.dtype) for i, a in enumerate(flat) if i != 7]
    held.append(pltpu.SMEM(flat[3].shape, flat[3].dtype))
    scratch = held + [
        pltpu.SemaphoreType.DMA((len(held),)),
        pltpu.VMEM((3 * groups, LANES), F32),
        pltpu.VMEM((8 * groups, LANES), F32),
        pltpu.VMEM((ROWS, elems), jnp.int32),
        pltpu.VMEM((ROWS, elems), jnp.int32),
        pltpu.VMEM((6 * ROWS, elems), F32),
        pltpu.VMEM((7 * groups, basis * elems), BF16),
        pltpu.VMEM((LANES, basis * elems), BF16),
        pltpu.VMEM((LANES, LANES), BF16),
        pltpu.VMEM((STEPS + 1, fields * ROWS, elems), F32),
        pltpu.VMEM((fields * faces * ROWS, elems), F32),
        pltpu.VMEM((8, elems), F32),
        pltpu.VMEM(((faces + 1) * ROWS, LANES), F32),
        pltpu.VMEM((8, LANES), F32),
        pltpu.VMEM((2 * ROWS, 2 * LANES), BF16),
        pltpu.VMEM((24, LANES), jnp.int32),
        pltpu.VMEM((3 * groups, LANES), F32),
        pltpu.VMEM((ROWS, elems), jnp.int32),
        pltpu.VMEM((basis * 8, LANES), F32),
        pltpu.VMEM((basis * 8, LANES), F32),
        pltpu.VMEM((2, 8 * ROWS, elems), BF16),
        pltpu.VMEM((2 * LANES, basis * elems), BF16),
        pltpu.VMEM((LANES, basis * elems), BF16),
        pltpu.VMEM((2, LANES, LANES), BF16),
        pltpu.VMEM((ROWS, elems), jnp.int32),
        pltpu.VMEM((STEPS, tiles, ROWS, LANES), F32),
        pltpu.VMEM((tiles, ROWS, LANES), F32),
        pltpu.VMEM((tiles, faces, ROWS, LANES), F32),
        pltpu.VMEM((tiles, 8, LANES), jnp.int32),
        pltpu.VMEM((tiles, 8, LANES), F32),
        pltpu.VMEM((8, LANES), jnp.int32),
        pltpu.VMEM((SWEEPS, 8, LANES), F32),
        pltpu.VMEM((SWEEPS, 4, 8, LANES), F32),
        pltpu.VMEM((STEPS, 4, ROWS, LANES), F32),
        pltpu.VMEM((STEPS, 4, ROWS, LANES), F32),
        pltpu.VMEM((max(len(rounds), 1), 1, LANES), F32),
        pltpu.VMEM((max(total, 1), 1, LANES), F32),
        pltpu.SemaphoreType.DMA((SWEEPS, 4)),
        pltpu.SemaphoreType.DMA((SWEEPS, 4)),
        pltpu.SemaphoreType.DMA((STEPS, 4)),
        pltpu.SemaphoreType.DMA((STEPS, 4)),
        pltpu.SemaphoreType.DMA((max(total, 1),)),
        pltpu.SemaphoreType.DMA((max(total, 1),)),
    ]
    coords, remapped = pl.pallas_call(
        functools.partial(kernel, parts, shifts, rounds, basis, elems, fields, faces, nodes),
        out_shape=(
            jax.ShapeDtypeStruct((3 * groups, LANES), F32),
            jax.ShapeDtypeStruct((fields * basis, halves, LANES), F32),
        ),
        in_specs=specs,
        out_specs=(vmem, vmem),
        scratch_shapes=scratch,
        compiler_params=pltpu.CompilerParams(
            collective_id=0, has_side_effects=True, vmem_limit_bytes=32 * 1024 * 1024
        ),
    )(*[a if i == 7 else pltpu.with_memory_space_constraint(a, pltpu.HBM) for i, a in enumerate(flat)])
    return coords.reshape(pos.shape), remapped.reshape(states.shape)


def solution(mesh):
    dom = lambda rank: P("dom", *([None] * (rank - 1)))
    in_specs = (
        dom(3), dom(4), dom(3), dom(3), dom(3), dom(3), dom(3), P("dom"),
        P(), P(), dom(3), P(), P(), P(),
    )
    return jax.shard_map(
        on_device, mesh=mesh, in_specs=in_specs, out_specs=(dom(3), dom(4)), check_vma=False
    )
```

```python
import functools
import math

import jax
import jax.numpy as jnp
from jax import lax
from jax.experimental import pallas as pl
from jax.experimental.pallas import tpu as pltpu
from jax.sharding import PartitionSpec as P

SWEEPS = 3
STEPS = 4
CFL = 0.4
F32 = jnp.float32
BF16 = jnp.bfloat16
HIGHEST = lax.Precision.HIGHEST
MESH = pl.DeviceIdType.MESH
LANES = 128
ROWS = 32
RADIX = 8


def rounds_of(parts):
    found, stride = [], 1
    while parts > 1:
        radix = max(r for r in range(1, RADIX + 1) if parts % r == 0)
        if radix == 1:
            radix = parts
        found.append((radix, stride))
        stride *= radix
        parts //= radix
    return found


def pick(table, index):
    return jnp.take_along_axis(table, index, axis=1, mode="promise_in_bounds")


def split(x):
    high = x.astype(BF16)
    low = (x - high.astype(F32)).astype(BF16)
    return high, low


def mm(a, b):
    return jnp.dot(a, b, preferred_element_type=F32)


def mm3(a, b):
    high, low = split(b)
    return mm(a[0], high) + (mm(a[1], high) + mm(a[0], low))


def mm_nt(a, b):
    return lax.dot_general(a, b, (((1,), (1,)), ((), ())), preferred_element_type=F32)


def iota(shape, dim):
    return lax.broadcasted_iota(jnp.int32, shape, dim)


def kernel(
    parts, shifts, rounds,
    basis, elems, fields, faces, nodes,
    pos_any, states_any, conn_any, send_nodes_any, recv_nodes_any, send_elems_any, neighbours_any, live,
    smooth_any, face_geo_any, rates_any, stiff_any, lift_any, mass_inv_any,
    out_c, out_u,
    x0_ref, states, conn, send_nodes, recv_nodes, send_elems, neighbours,
    smooth, face_geo, rates, stiff, lift, mass_inv, sent_smem, in_sem,
    x_ref, s_ref, lo_ref, hi_ref, y_ref, z_ref, b_ref, rb_ref,
    u_ref, nb_ref, rate_ref, pad_ref, fg_ref, w_ref, idx_ref,
    mv_ref, cm_ref, ka_ref, kb_ref, oh_ref, hs_ref, gr_ref, tt_ref, sl_ref, st_ref, gt_ref, nl_ref, nbs_ref, rs_ref, nbp_ref, ds_ref,
    v_send, v_recv, g_send, g_recv, m_send, m_recv,
    vs_sem, vr_sem, gs_sem, gr_sem, ms_sem, mr_sem,
):
    me = lax.axis_index("dom")
    groups = nodes // LANES
    halves = elems // LANES
    shared = send_nodes.shape[1]
    ghosts = send_elems.shape[1]
    slots = LANES // ghosts

    sources = (
        conn_any, pos_any, send_nodes_any, recv_nodes_any, smooth_any, send_elems_any, states_any,
        neighbours_any, rates_any, face_geo_any, mass_inv_any, stiff_any, lift_any, send_nodes_any,
    )
    places = (
        conn, x0_ref, send_nodes, recv_nodes, smooth, send_elems, states,
        neighbours, rates, face_geo, mass_inv, stiff, lift, sent_smem,
    )
    loads = [
        pltpu.make_async_copy(a, b, in_sem.at[i]) for i, (a, b) in enumerate(zip(sources, places))
    ]
    for one in loads:
        one.start()

    partners = []
    for radix, stride in rounds:
        digit = lax.rem(me // stride, radix)
        partners.append(
            [me + (lax.rem(digit + j, radix) - digit) * stride for j in range(1, radix)]
        )
    targets = [lax.rem(me + o + parts, parts) for o in shifts]

    barrier = pltpu.get_barrier_semaphore()
    greeted = targets + [t for one in partners for t in one]
    for t in greeted:
        pl.semaphore_signal(barrier, inc=1, device_id=(t,), device_id_type=MESH)

    def node_copy(sweep, k):
        return pltpu.make_async_remote_copy(
            src_ref=v_send.at[sweep], dst_ref=v_recv.at[sweep, k],
            send_sem=vs_sem.at[sweep, k], recv_sem=vr_sem.at[sweep, k],
            device_id=(targets[k],), device_id_type=MESH,
        )

    def ghost_copy(step, k):
        return pltpu.make_async_remote_copy(
            src_ref=g_send.at[step, k], dst_ref=g_recv.at[step, k],
            send_sem=gs_sem.at[step, k], recv_sem=gr_sem.at[step, k],
            device_id=(targets[k],), device_id_type=MESH,
        )

    def most_copy(r, j):
        at = sum(len(p) for p in partners[:r]) + j
        return pltpu.make_async_remote_copy(
            src_ref=m_send.at[r], dst_ref=m_recv.at[at],
            send_sem=ms_sem.at[at], recv_sem=mr_sem.at[at],
            device_id=(partners[r][j],), device_id_type=MESH,
        )

    lane = iota((8, LANES), 1)
    row = iota((8, LANES), 0)
    slot_of = iota((ROWS, LANES), 1) // ghosts
    tiles = (fields + 1) // 2

    idx_ref[...] = jnp.zeros(idx_ref.shape, jnp.int32)
    lo_ref[...] = jnp.zeros(lo_ref.shape, jnp.int32)
    hi_ref[...] = jnp.zeros(hi_ref.shape, jnp.int32)
    s_ref[...] = jnp.zeros(s_ref.shape, F32)
    u_ref[0] = jnp.zeros(u_ref.shape[1:], F32)
    cm_ref[...] = jnp.full(cm_ref.shape, -1, jnp.int32)
    ka_ref[...] = jnp.zeros(ka_ref.shape, F32)
    kb_ref[...] = jnp.zeros(kb_ref.shape, F32)
    pad_ref[...] = jnp.zeros(pad_ref.shape, F32)
    fg_ref[...] = jnp.zeros(fg_ref.shape, F32)
    nbp_ref[...] = jnp.zeros(nbp_ref.shape, jnp.int32)
    rate_ref[...] = jnp.zeros(rate_ref.shape, F32)
    alive = iota((1, elems), 1) < live[0]
    for one in loads[:6]:
        one.wait()

    pad_ref[0:basis, 0:basis] = smooth[...]
    smooth_parts = split(pad_ref[0:ROWS, 0:ROWS])
    idx_ref[0:4, 0:shared] = send_nodes[...]
    idx_ref[8:12, 0:shared] = recv_nodes[...]
    idx_ref[16:20, 0:ghosts] = send_elems[...]

    def flat(block, width, count):
        spread = pick(block, lax.rem(lane, width))
        kept = jnp.where(lax.rem(lane // width, count) == row, spread, 0)
        return jnp.sum(kept, axis=0, keepdims=True)

    sent_nodes = flat(idx_ref[0:8, :], shared, 4)
    got_nodes = flat(idx_ref[8:16, :], shared, 4)

    for h in range(halves):
        part = conn[:, h, :]
        lo_ref[0:basis, h * LANES : (h + 1) * LANES] = part & (LANES - 1)
        hi_ref[0:basis, h * LANES : (h + 1) * LANES] = part >> 7
        cm_ref[0:basis, h * LANES : (h + 1) * LANES] = part
    cm_ref[...] = jnp.where(alive, cm_ref[...], -1)

    sub_lo = iota((LANES, elems), 0)
    sub_hi = iota((groups, elems), 0)
    one_lo, one_hi = jnp.float32(1.0), jnp.float32(1.0)
    for a in range(basis):
        at = pl.ds(a * elems, elems)
        b_ref[:, at] = jnp.where(sub_lo == lo_ref[a : a + 1, :], one_lo, 0.0).astype(BF16)

    def corners(row_of, count):
        result = []
        for c in range(count):
            cols = []
            for h in range(halves):
                low = lo_ref[:, h * LANES : (h + 1) * LANES]
                high = hi_ref[:, h * LANES : (h + 1) * LANES]
                value = None
                for g in range(groups):
                    source = jnp.broadcast_to(row_of(c * groups + g), (ROWS, LANES))
                    got = pick(source, low)
                    value = got if value is None else jnp.where(high == g, got, value)
                cols.append(value)
            result.append(jnp.concatenate(cols, axis=1))
        return result

    def scatter(ys, counting=False):
        for c in range(3):
            y_high = ys[c].astype(BF16).astype(F32)
            y_ref[c * ROWS : (c + 1) * ROWS, :] = y_high
            y_ref[(3 + c) * ROWS : (4 + c) * ROWS, :] = ys[c] - y_high
        for a in range(basis):
            at = pl.ds(a * elems, elems)
            chosen = jnp.where(alive, hi_ref[a : a + 1, :], groups) == sub_hi
            for i in range(6):
                z_ref[i * groups : (i + 1) * groups, at] = jnp.where(
                    chosen, y_ref[i * ROWS + a : i * ROWS + a + 1, :], 0.0
                ).astype(BF16)
            if counting:
                z_ref[6 * groups : 7 * groups, at] = jnp.where(chosen, one_hi, 0.0).astype(BF16)
        rows = (7 if counting else 6) * groups
        both = mm_nt(z_ref[0:rows, :], b_ref[...])
        result = both[0 : 3 * groups] + both[3 * groups : 6 * groups]
        return (result, both[6 * groups :]) if counting else result

    s_low = jnp.broadcast_to(sent_nodes & (LANES - 1), (8, LANES))
    s_high = jnp.broadcast_to(sent_nodes >> 7, (8, LANES))

    def at_sent(sums):
        for c in range(3):
            for g in range(groups):
                r = c * groups + g
                s_ref[g * 8 + c : g * 8 + c + 1, :] = sums[r : r + 1, :]
        picked = jnp.zeros((8, LANES), F32)
        for g in range(groups):
            picked = jnp.where(s_high == g, pick(s_ref[g * 8 : g * 8 + 8, :], s_low), picked)
        return jnp.where(row < 3, picked, 0.0)

    def smoothed(near):
        return [mm3(smooth_parts, near[c]) for c in range(3)]

    def send_sums(sweep, value):
        v_send[sweep] = value
        for k in range(4):
            node_copy(sweep, k).start()

    sums, count = scatter(smoothed(corners(lambda r: x0_ref[r : r + 1, :], 3)), True)
    first_sent = at_sent(sums)
    pl.semaphore_wait(barrier, len(greeted))
    send_sums(0, first_sent)

    for one in loads[6:]:
        one.wait()
    sent_elems = jnp.broadcast_to(flat(idx_ref[16:24, :], ghosts, 4), (8, LANES))
    sent_tile = [sent_elems]
    for t in range(1, tiles):
        sent_tile.append(pltpu.roll(sent_elems, ghosts * t, 1))
    first_of = [((slot_of + (slots - t)) & (slots - 1)) < 4 for t in range(tiles)]

    def choose(level, t, low, far):
        result = None
        for v in range(2 * t, min(2 * t + 2, fields)):
            got = None
            for h in range(halves):
                one = pick(u_ref[level, v * ROWS : (v + 1) * ROWS, h * LANES : (h + 1) * LANES], low)
                got = one if got is None else jnp.where(far == h, one, got)
            result = got if result is None else jnp.where(first_of[t], result, got)
        return result

    def send_ghosts(step):
        for k in range(4):
            tile = st_ref[step, 0]
            for t in range(1, tiles):
                tile = jnp.where(((slot_of + (slots - k)) & 3) == t, st_ref[step, t], tile)
            g_send[step, k] = tile
        for k in range(4):
            ghost_copy(step, k).start()

    got_lo, got_hi = got_nodes & (LANES - 1), got_nodes >> 7
    rb_ref[...] = jnp.where(iota((LANES, LANES), 0) == got_lo, one_lo, 0.0).astype(BF16)
    got_mask = iota((groups, LANES), 0) == got_hi
    count = count + mm_nt(jnp.where(got_mask, one_hi, 0.0).astype(BF16), rb_ref[...])
    half_inv = 0.5 / jnp.maximum(count, 1.0)
    hi_at_got = jnp.zeros((8, LANES), F32)
    got_lo8 = jnp.broadcast_to(got_lo, (8, LANES))
    got_hi8 = jnp.broadcast_to(got_hi, (8, LANES))
    for g in range(groups):
        hi_at_got = jnp.where(
            got_hi8 == g, pick(jnp.broadcast_to(half_inv[g : g + 1, :], (8, LANES)), got_lo8), hi_at_got
        )
    half_inv = jnp.concatenate([half_inv] * 3, axis=0)


    square = (LANES, LANES)
    got_row = jnp.broadcast_to(got_nodes, square)
    got_col = jnp.transpose(got_row)
    got_wide = jnp.concatenate([got_col] * halves, axis=1)
    for a in range(basis):
        node = cm_ref[a : a + 1, :]
        gr_ref[:, pl.ds(a * elems, elems)] = jnp.where(got_wide == node, one_lo, 0.0).astype(BF16)
    turned = jnp.transpose(pad_ref[0:LANES, :])[0:ROWS, :]
    for i in range(8):
        place = ka_ref if i < 4 else kb_ref
        placed = turned if i % 4 == 0 else pltpu.roll(turned, ROWS * (i % 4), 1)
        place[pl.ds(i, basis, stride=8), :] = placed[0:basis, :]
    k8_high, k8_low = split(jnp.concatenate([ka_ref[...], kb_ref[...]], axis=1))
    for pair in range(LANES // 16):
        both = []
        for part in range(2):
            for i in range(8):
                slot = pair * 16 + part * 8 + i
                node = sent_smem[slot // shared, slot % shared]
                oh_ref[part, i * ROWS : (i + 1) * ROWS, :] = jnp.where(
                    cm_ref[...] == node, one_lo, 0.0
                ).astype(BF16)
            both.append(mm(k8_high, oh_ref[part]) + mm(k8_low, oh_ref[part]))
        for b in range(basis):
            block = jnp.concatenate([one[b * 8 : (b + 1) * 8] for one in both], axis=0)
            high, low = split(block)
            at = pl.ds(b * elems, elems)
            hs_ref[pair * 16 : (pair + 1) * 16, at] = high
            hs_ref[LANES + pair * 16 : LANES + (pair + 1) * 16, at] = low
    response = mm_nt(hs_ref[...], gr_ref[...])
    response = split((response[0:LANES] + response[LANES:]) * hi_at_got[0:1, :])
    for i in range(2):
        tt_ref[i] = response[i]

    x_ref[...] = 0.5 * x0_ref[...] + sums * half_inv
    ahead = scatter(smoothed(corners(lambda r: x_ref[r : r + 1, :], 3)))
    ahead_sent = at_sent(ahead)

    def to_sent(arrived):
        high, low = split(arrived)
        return mm_nt(high, tt_ref[0]) + (mm_nt(low, tt_ref[0]) + mm_nt(high, tt_ref[1]))

    def prepare_slots():
        marked = jnp.where((got_col & (LANES - 1)) == iota(square, 1), iota(square, 0) + 1, 0)
        col_hi = got_col >> 7
        table = [
            jnp.max(jnp.where(col_hi == g, marked, 0), axis=0, keepdims=True) for g in range(groups)
        ]
        sl_ref[...] = corners(lambda r: table[r], 1)[0]

    def received(sweep):
        for k in range(4):
            node_copy(sweep, k).wait_recv()
        arrived = v_recv[sweep, 0]
        for k in range(1, 4):
            arrived = jnp.where(lane // shared == k, v_recv[sweep, k], arrived)
        return arrived

    same = jnp.where(got_row == got_col, one_lo, 0.0).astype(BF16)

    def gathered(arrived):
        high, low = split(arrived)
        spread = (mm(high, same) + mm(low, same)) * hi_at_got
        near = []
        for c in range(3):
            cols = []
            for h in range(halves):
                index = sl_ref[:, h * LANES : (h + 1) * LANES]
                source = jnp.broadcast_to(spread[c : c + 1, :], (ROWS, LANES))
                cols.append(jnp.where(index > 0, pick(source, (index + (LANES - 1)) & (LANES - 1)), 0.0))
            near.append(jnp.concatenate(cols, axis=1))
        return near

    def injected(arrived):
        arr_high = arrived.astype(BF16).astype(F32)
        arr_low = arrived - arr_high
        pieces = [
            jnp.where(got_mask, part[c : c + 1, :], 0.0).astype(BF16)
            for part in (arr_high, arr_low) for c in range(3)
        ]
        both = mm_nt(jnp.concatenate(pieces, axis=0), rb_ref[...])
        return (both[0 : 3 * groups] + both[3 * groups :]) * half_inv

    def prepare_weights():
        for i in range(faces + 1):
            matrix = stiff[...] if i == 0 else lift[i - 1]
            pad_ref[i * ROWS : i * ROWS + basis, 0:basis] = jnp.dot(
                mass_inv[...], matrix, precision=HIGHEST, preferred_element_type=F32
            )
        wide = []
        for first in range(0, faces + 1, 4):
            total = None
            for i in range(first, min(first + 4, faces + 1)):
                block = pad_ref[i * ROWS : (i + 1) * ROWS, :]
                if i > first:
                    block = pltpu.roll(block, ROWS * (i - first), 1)
                total = block if total is None else total + block
            wide.append(total)
        w_high, w_low = split(jnp.concatenate(wide, axis=1))
        w_ref[0:ROWS, :] = w_high
        w_ref[ROWS : 2 * ROWS, :] = w_low
        for c in range(3):
            fg_ref[0:faces, c * ROWS : c * ROWS + basis] = face_geo[:, c, :]

    def gather_local(step):
        for v in range(fields):
            for h in range(halves):
                for f in range(faces):
                    which = jnp.broadcast_to(neighbours[f, h : h + 1, :], (ROWS, LANES))
                    low, far = which & (LANES - 1), which >> 7
                    got = None
                    for s in range(halves):
                        other = pick(u_ref[step, v * ROWS : (v + 1) * ROWS, s * LANES : (s + 1) * LANES], low)
                        got = other if got is None else jnp.where(far == s, other, got)
                    r = (v * faces + f) * ROWS
                    nb_ref[r : r + ROWS, h * LANES : (h + 1) * LANES] = got

    def gather_sent(step):
        for t in range(tiles):
            for f in range(faces):
                which = jnp.broadcast_to(nbs_ref[t, f : f + 1, :], (ROWS, LANES))
                nl_ref[t, f] = choose(step, t, which & (LANES - 1), which >> 7)

    def wait_ghosts(step):
        for k in range(4):
            ghost_copy(step, k).wait_recv()
        for t in range(tiles):
            tile = g_recv[step, 0]
            for k in range(1, 4):
                tile = jnp.where(((slot_of + (slots - t)) & 3) == k, g_recv[step, k], tile)
            gt_ref[t] = tile

    depth = (faces + 1) * ROWS

    def times(stack):
        high, low = split(jnp.concatenate(stack, axis=0))
        first = mm(w_ref[:, 0:depth], high)
        return first[0:ROWS] + (first[ROWS:] + mm(w_ref[0:ROWS, 0:depth], low))

    def prepare_sent():
        for f in range(faces):
            cols = []
            for t in range(tiles):
                cols.append(neighbour_of_sent(0, t, f) - st_ref[0, t])
            ds_ref[f + 1] = one_face(f + 1, jnp.concatenate(cols, axis=1))
        ds_ref[0] = one_face(0, jnp.concatenate([st_ref[0, t] for t in range(tiles)], axis=1))

    def one_face(i, value):
        at = i * ROWS
        return mm3((w_ref[0:ROWS, at : at + ROWS], w_ref[ROWS : 2 * ROWS, at : at + ROWS]), value)

    def kept_sent(t):
        return jnp.where(sent_tile[t][0:1, :] < live[0], 1.0, 0.0)

    def first_sent_step():
        for t in range(tiles):
            at = pl.ds(t * LANES, LANES)
            new = ds_ref[0, :, at]
            for f in range(faces):
                new = new + rs_ref[t, f : f + 1, :] * ds_ref[f + 1, :, at]
            st_ref[1, t] = new * kept_sent(t)

    def neighbour_of_sent(step, t, f):
        which = jnp.broadcast_to(nbs_ref[t, f : f + 1, :], (ROWS, LANES))
        at = which + jnp.where(first_of[t], ghosts * t, ghosts * (t + 4))
        return jnp.where(which >= elems, pick(gt_ref[t], at & (LANES - 1)), nl_ref[t, f])

    def advance_sent(step):
        stack = [jnp.concatenate([st_ref[step, t] for t in range(tiles)], axis=1)]
        for f in range(faces):
            cols = []
            for t in range(tiles):
                got = neighbour_of_sent(step, t, f)
                cols.append(rs_ref[t, f : f + 1, :] * (got - st_ref[step, t]))
            stack.append(jnp.concatenate(cols, axis=1))
        new = times(stack)
        for t in range(tiles):
            st_ref[step + 1, t] = new[:, t * LANES : (t + 1) * LANES] * kept_sent(t)

    def change_of(v, step):
        u = u_ref[step, v * ROWS : (v + 1) * ROWS, :]
        stack = [u]
        for f in range(faces):
            cols = []
            r = (v * faces + f) * ROWS
            for h in range(halves):
                which = jnp.broadcast_to(neighbours[f, h : h + 1, :], (ROWS, LANES))
                got = pick(gt_ref[v // 2], (which + ghosts * (v // 2 + 4 * (v % 2))) & (LANES - 1))
                cols.append(jnp.where(which >= elems, got, nb_ref[r : r + ROWS, h * LANES : (h + 1) * LANES]))
            stack.append(rate_ref[f : f + 1, :] * (jnp.concatenate(cols, axis=1) - u))
        return times(stack)

    def finish_round(r, most):
        at = sum(len(p) for p in partners[:r])
        tile = m_send[r]
        for j in range(len(partners[r])):
            most_copy(r, j).wait_recv()
            tile = jnp.maximum(tile, m_recv[at + j])
        most = tile[0:1, 0:1]
        if r + 1 < len(partners):
            m_send[r + 1] = jnp.broadcast_to(most, (1, LANES))
            for j in range(len(partners[r + 1])):
                most_copy(r + 1, j).start()
        return most

    for sweep in range(SWEEPS - 1):
        arrived = received(sweep)
        send_sums(sweep + 1, ahead_sent + to_sent(arrived))
        if sweep == 0:
            for v in range(fields):
                for h in range(halves):
                    u_ref[0, v * ROWS : v * ROWS + basis, h * LANES : (h + 1) * LANES] = states[
                        v * basis : (v + 1) * basis, h, :
                    ]
            for t in range(tiles):
                which = jnp.broadcast_to(sent_tile[t][0:1, :], (ROWS, LANES))
                st_ref[0, t] = choose(0, t, which & (LANES - 1), which >> 7)
            send_ghosts(0)
            prepare_slots()
        ys = smoothed(gathered(arrived))
        x_ref[...] = x_ref[...] + injected(arrived)
        sums = ahead + scatter(ys)
        x_ref[...] = 0.5 * x_ref[...] + sums * half_inv
        if sweep < SWEEPS - 2:
            ahead = scatter(smoothed(corners(lambda r: x_ref[r : r + 1, :], 3)))
            ahead_sent = at_sent(ahead)

    prepare_weights()
    geo_parts = split(fg_ref[:, 0 : 3 * ROWS])
    mv_ref[...] = x_ref[...] - x0_ref[...]
    projected = mm3(geo_parts, jnp.concatenate(corners(lambda r: mv_ref[r : r + 1, :], 3), axis=0))
    base = jnp.concatenate([rates[:, h, :] for h in range(halves)], axis=1)
    keep = jnp.where(alive, 1.0, 0.0)
    for t in range(tiles):
        low, far = sent_tile[t] & (LANES - 1), sent_tile[t] >> 7
        got = jnp.zeros((8, LANES), jnp.int32)
        for h in range(halves):
            nbp_ref[0:faces, :] = neighbours[:, h, :]
            got = jnp.where(far == h, pick(nbp_ref[...], low), got)
        nbs_ref[t] = got
    gather_sent(0)
    gather_local(0)
    wait_ghosts(0)
    prepare_sent()

    arrived = received(SWEEPS - 1)
    near = gathered(arrived)
    projected = projected + mm3(geo_parts, jnp.concatenate(near, axis=0))
    rate = base * (1.0 + 0.5 * jnp.tanh(projected[0:faces])) * keep
    rate_ref[0:faces, :] = rate
    for t in range(tiles):
        low, far = sent_tile[t] & (LANES - 1), sent_tile[t] >> 7
        got = jnp.zeros((8, LANES), F32)
        for h in range(halves):
            got = jnp.where(far == h, pick(rate_ref[:, h * LANES : (h + 1) * LANES], low), got)
        rs_ref[t] = got
    first_sent_step()
    send_ghosts(1)
    most = jnp.max(jnp.sum(rate, axis=0, keepdims=True), axis=1, keepdims=True)
    m_send[0] = jnp.broadcast_to(most, (1, LANES))
    for j in range(len(partners[0]) if rounds else 0):
        most_copy(0, j).start()
    out_c[...] = x_ref[...] + injected(arrived)

    for step in range(STEPS - 1):
        for v in range(fields):
            u_ref[step + 1, v * ROWS : (v + 1) * ROWS, :] = keep * change_of(v, step)
        if step + 2 < STEPS:
            gather_sent(step + 1)
        gather_local(step + 1)
        if step == STEPS - 2:
            for r in range(step, len(partners)):
                most = finish_round(r, most)
            scale = jnp.broadcast_to(CFL / most, (ROWS, elems))
            for v in range(fields):
                total = math.comb(STEPS, STEPS - 1) * u_ref[STEPS - 1, v * ROWS : (v + 1) * ROWS, :]
                for k in range(STEPS - 2, -1, -1):
                    total = math.comb(STEPS, k) * u_ref[k, v * ROWS : (v + 1) * ROWS, :] + scale * total
                u_ref[STEPS, v * ROWS : (v + 1) * ROWS, :] = total
        wait_ghosts(step + 1)
        if step + 2 < STEPS:
            advance_sent(step + 1)
            send_ghosts(step + 2)
        if step < min(STEPS - 2, len(partners)):
            most = finish_round(step, most)
    scale = keep * (scale * scale) * (scale * scale)
    for v in range(fields):
        new = u_ref[STEPS, v * ROWS : (v + 1) * ROWS, :] + scale * change_of(v, STEPS - 1)
        for h in range(halves):
            out_u[v * basis : (v + 1) * basis, h, :] = new[0:basis, h * LANES : (h + 1) * LANES]

    for sweep in range(SWEEPS):
        for k in range(4):
            node_copy(sweep, k).wait_send()
    for step in range(STEPS):
        for k in range(4):
            ghost_copy(step, k).wait_send()
    for r, one in enumerate(partners):
        for j in range(len(one)):
            most_copy(r, j).wait_send()


def hand_over(coords, remapped, out_c, out_u, sem):
    moves = [
        pltpu.make_async_copy(remapped, out_u, sem.at[0]),
        pltpu.make_async_copy(coords, out_c, sem.at[1]),
    ]
    for one in moves:
        one.start()
    for one in moves:
        one.wait()


def on_device(*args):
    pos, states, conn = args[:3]
    parts = lax.axis_size("dom")
    w = max(parts // 8, 1)
    shifts = (1, -1, w, -w)
    rounds = rounds_of(parts)
    total = sum(r - 1 for r, _ in rounds)
    basis, elems = conn.shape[1:]
    fields, faces = states.shape[1], args[6].shape[1]
    groups = pos.shape[2] // LANES
    nodes = pos.shape[2]
    halves = elems // LANES
    tiles = (fields + 1) // 2
    flat = list(args)
    for i, rows in ((0, 3 * groups), (1, fields * basis * halves), (2, basis * halves), (6, faces * halves), (10, faces * halves)):
        flat[i] = args[i].reshape(rows, LANES) if i == 0 else args[i].reshape(rows // halves, halves, LANES)
    for i in (3, 4, 5):
        flat[i] = args[i][0]
    vmem = pl.BlockSpec(memory_space=pltpu.VMEM)
    smem = pl.BlockSpec(memory_space=pltpu.SMEM)
    hbm = pl.BlockSpec(memory_space=pl.ANY)
    specs = [smem if i == 7 else hbm for i in range(len(args))]
    held = [pltpu.VMEM(a.shape, a.dtype) for i, a in enumerate(flat) if i != 7]
    held.append(pltpu.SMEM(flat[3].shape, flat[3].dtype))
    scratch = held + [
        pltpu.SemaphoreType.DMA((len(held),)),
        pltpu.VMEM((3 * groups, LANES), F32),
        pltpu.VMEM((8 * groups, LANES), F32),
        pltpu.VMEM((ROWS, elems), jnp.int32),
        pltpu.VMEM((ROWS, elems), jnp.int32),
        pltpu.VMEM((6 * ROWS, elems), F32),
        pltpu.VMEM((7 * groups, basis * elems), BF16),
        pltpu.VMEM((LANES, basis * elems), BF16),
        pltpu.VMEM((LANES, LANES), BF16),
        pltpu.VMEM((STEPS + 1, fields * ROWS, elems), F32),
        pltpu.VMEM((fields * faces * ROWS, elems), F32),
        pltpu.VMEM((8, elems), F32),
        pltpu.VMEM(((faces + 1) * ROWS, LANES), F32),
        pltpu.VMEM((8, LANES), F32),
        pltpu.VMEM((2 * ROWS, 2 * LANES), BF16),
        pltpu.VMEM((24, LANES), jnp.int32),
        pltpu.VMEM((3 * groups, LANES), F32),
        pltpu.VMEM((ROWS, elems), jnp.int32),
        pltpu.VMEM((basis * 8, LANES), F32),
        pltpu.VMEM((basis * 8, LANES), F32),
        pltpu.VMEM((2, 8 * ROWS, elems), BF16),
        pltpu.VMEM((2 * LANES, basis * elems), BF16),
        pltpu.VMEM((LANES, basis * elems), BF16),
        pltpu.VMEM((2, LANES, LANES), BF16),
        pltpu.VMEM((ROWS, elems), jnp.int32),
        pltpu.VMEM((STEPS, tiles, ROWS, LANES), F32),
        pltpu.VMEM((tiles, ROWS, LANES), F32),
        pltpu.VMEM((tiles, faces, ROWS, LANES), F32),
        pltpu.VMEM((tiles, 8, LANES), jnp.int32),
        pltpu.VMEM((tiles, 8, LANES), F32),
        pltpu.VMEM((8, LANES), jnp.int32),
        pltpu.VMEM((faces + 1, ROWS, tiles * LANES), F32),
        pltpu.VMEM((SWEEPS, 8, LANES), F32),
        pltpu.VMEM((SWEEPS, 4, 8, LANES), F32),
        pltpu.VMEM((STEPS, 4, ROWS, LANES), F32),
        pltpu.VMEM((STEPS, 4, ROWS, LANES), F32),
        pltpu.VMEM((max(len(rounds), 1), 1, LANES), F32),
        pltpu.VMEM((max(total, 1), 1, LANES), F32),
        pltpu.SemaphoreType.DMA((SWEEPS, 4)),
        pltpu.SemaphoreType.DMA((SWEEPS, 4)),
        pltpu.SemaphoreType.DMA((STEPS, 4)),
        pltpu.SemaphoreType.DMA((STEPS, 4)),
        pltpu.SemaphoreType.DMA((max(total, 1),)),
        pltpu.SemaphoreType.DMA((max(total, 1),)),
    ]
    coords, remapped = pl.pallas_call(
        functools.partial(kernel, parts, shifts, rounds, basis, elems, fields, faces, nodes),
        out_shape=(
            jax.ShapeDtypeStruct((3 * groups, LANES), F32),
            jax.ShapeDtypeStruct((fields * basis, halves, LANES), F32),
        ),
        in_specs=specs,
        out_specs=(vmem, vmem),
        scratch_shapes=scratch,
        compiler_params=pltpu.CompilerParams(
            collective_id=0, has_side_effects=True, vmem_limit_bytes=32 * 1024 * 1024
        ),
    )(*[a if i == 7 else pltpu.with_memory_space_constraint(a, pltpu.HBM) for i, a in enumerate(flat)])
    coords, remapped = pl.pallas_call(
        hand_over,
        out_shape=(pltpu.HBM(coords.shape, F32), pltpu.HBM(remapped.shape, F32)),
        in_specs=[vmem, vmem],
        out_specs=(hbm, hbm),
        scratch_shapes=[pltpu.SemaphoreType.DMA((2,))],
        compiler_params=pltpu.CompilerParams(vmem_limit_bytes=1024 * 1024),
    )(coords, remapped)
    return coords.reshape(pos.shape), remapped.reshape(states.shape)


def solution(mesh):
    dom = lambda rank: P("dom", *([None] * (rank - 1)))
    in_specs = (
        dom(3), dom(4), dom(3), dom(3), dom(3), dom(3), dom(3), P("dom"),
        P(), P(), dom(3), P(), P(), P(),
    )
    return jax.shard_map(
        on_device, mesh=mesh, in_specs=in_specs, out_specs=(dom(3), dom(4)), check_vma=False
    )
```

```python
import functools
import math

import jax
import jax.numpy as jnp
from jax import lax
from jax.experimental import pallas as pl
from jax.experimental.pallas import tpu as pltpu
from jax.sharding import PartitionSpec as P

SWEEPS = 3
STEPS = 4
CFL = 0.4
F32 = jnp.float32
BF16 = jnp.bfloat16
HIGHEST = lax.Precision.HIGHEST
MESH = pl.DeviceIdType.MESH
LANES = 128
ROWS = 32
RADIX = 8


def rounds_of(parts):
    found, stride = [], 1
    while parts > 1:
        radix = max(r for r in range(1, RADIX + 1) if parts % r == 0)
        if radix == 1:
            radix = parts
        found.append((radix, stride))
        stride *= radix
        parts //= radix
    return found


def pick(table, index):
    return jnp.take_along_axis(table, index, axis=1, mode="promise_in_bounds")


def split(x):
    high = x.astype(BF16)
    low = (x - high.astype(F32)).astype(BF16)
    return high, low


def mm(a, b):
    return jnp.dot(a, b, preferred_element_type=F32)


def mm3(a, b):
    high, low = split(b)
    return mm(a[0], high) + (mm(a[1], high) + mm(a[0], low))


def mm_nt(a, b):
    return lax.dot_general(a, b, (((1,), (1,)), ((), ())), preferred_element_type=F32)


def iota(shape, dim):
    return lax.broadcasted_iota(jnp.int32, shape, dim)


def kernel(
    parts, shifts, rounds,
    basis, elems, fields, faces, nodes,
    pos_any, states_any, conn_any, send_nodes_any, recv_nodes_any, send_elems_any, neighbours_any, live,
    smooth_any, face_geo_any, rates_any, stiff_any, lift_any, mass_inv_any,
    out_c, out_u,
    x0_ref, states, conn, send_nodes, recv_nodes, send_elems, neighbours,
    smooth, face_geo, rates, stiff, lift, mass_inv, sent_smem, in_sem,
    x_ref, s_ref, lo_ref, hi_ref, y_ref, z_ref, b_ref, rb_ref,
    u_ref, nb_ref, rate_ref, pad_ref, fg_ref, w_ref, idx_ref,
    mv_ref, cm_ref, ka_ref, kb_ref, oh_ref, hs_ref, gr_ref, tt_ref, sl_ref, st_ref, gt_ref, nl_ref, nbs_ref, rs_ref, nbp_ref, ds_ref,
    v_send, v_recv, g_send, g_recv, m_send, m_recv,
    vs_sem, vr_sem, gs_sem, gr_sem, ms_sem, mr_sem,
):
    me = lax.axis_index("dom")
    groups = nodes // LANES
    halves = elems // LANES
    shared = send_nodes.shape[1]
    ghosts = send_elems.shape[1]
    slots = LANES // ghosts

    sources = (
        conn_any, pos_any, send_nodes_any, recv_nodes_any, smooth_any, send_elems_any, states_any,
        neighbours_any, rates_any, face_geo_any, mass_inv_any, stiff_any, lift_any, send_nodes_any,
    )
    places = (
        conn, x0_ref, send_nodes, recv_nodes, smooth, send_elems, states,
        neighbours, rates, face_geo, mass_inv, stiff, lift, sent_smem,
    )
    loads = [
        pltpu.make_async_copy(a, b, in_sem.at[i]) for i, (a, b) in enumerate(zip(sources, places))
    ]
    for one in loads:
        one.start()

    partners = []
    for radix, stride in rounds:
        digit = lax.rem(me // stride, radix)
        partners.append(
            [me + (lax.rem(digit + j, radix) - digit) * stride for j in range(1, radix)]
        )
    targets = [lax.rem(me + o + parts, parts) for o in shifts]

    barrier = pltpu.get_barrier_semaphore()
    greeted = targets + [t for one in partners for t in one]
    for t in greeted:
        pl.semaphore_signal(barrier, inc=1, device_id=(t,), device_id_type=MESH)

    def node_copy(sweep, k):
        return pltpu.make_async_remote_copy(
            src_ref=v_send.at[sweep], dst_ref=v_recv.at[sweep, k],
            send_sem=vs_sem.at[sweep, k], recv_sem=vr_sem.at[sweep, k],
            device_id=(targets[k],), device_id_type=MESH,
        )

    def ghost_copy(step, k):
        return pltpu.make_async_remote_copy(
            src_ref=g_send.at[step, k], dst_ref=g_recv.at[step, k],
            send_sem=gs_sem.at[step, k], recv_sem=gr_sem.at[step, k],
            device_id=(targets[k],), device_id_type=MESH,
        )

    def most_copy(r, j):
        at = sum(len(p) for p in partners[:r]) + j
        return pltpu.make_async_remote_copy(
            src_ref=m_send.at[r], dst_ref=m_recv.at[at],
            send_sem=ms_sem.at[at], recv_sem=mr_sem.at[at],
            device_id=(partners[r][j],), device_id_type=MESH,
        )

    lane = iota((8, LANES), 1)
    row = iota((8, LANES), 0)
    slot_of = iota((ROWS, LANES), 1) // ghosts
    tiles = (fields + 1) // 2

    idx_ref[...] = jnp.zeros(idx_ref.shape, jnp.int32)
    lo_ref[...] = jnp.zeros(lo_ref.shape, jnp.int32)
    hi_ref[...] = jnp.zeros(hi_ref.shape, jnp.int32)
    s_ref[...] = jnp.zeros(s_ref.shape, F32)
    u_ref[0] = jnp.zeros(u_ref.shape[1:], F32)
    cm_ref[...] = jnp.full(cm_ref.shape, -1, jnp.int32)
    ka_ref[...] = jnp.zeros(ka_ref.shape, F32)
    kb_ref[...] = jnp.zeros(kb_ref.shape, F32)
    pad_ref[...] = jnp.zeros(pad_ref.shape, F32)
    fg_ref[...] = jnp.zeros(fg_ref.shape, F32)
    nbp_ref[...] = jnp.zeros(nbp_ref.shape, jnp.int32)
    rate_ref[...] = jnp.zeros(rate_ref.shape, F32)
    alive = iota((1, elems), 1) < live[0]
    for one in loads[:6]:
        one.wait()

    pad_ref[0:basis, 0:basis] = smooth[...]
    smooth_parts = split(pad_ref[0:ROWS, 0:ROWS])
    idx_ref[0:4, 0:shared] = send_nodes[...]
    idx_ref[8:12, 0:shared] = recv_nodes[...]
    idx_ref[16:20, 0:ghosts] = send_elems[...]

    def flat(block, width, count):
        spread = pick(block, lax.rem(lane, width))
        kept = jnp.where(lax.rem(lane // width, count) == row, spread, 0)
        return jnp.sum(kept, axis=0, keepdims=True)

    sent_nodes = flat(idx_ref[0:8, :], shared, 4)
    got_nodes = flat(idx_ref[8:16, :], shared, 4)

    for h in range(halves):
        part = conn[:, h, :]
        lo_ref[0:basis, h * LANES : (h + 1) * LANES] = part & (LANES - 1)
        hi_ref[0:basis, h * LANES : (h + 1) * LANES] = part >> 7
        cm_ref[0:basis, h * LANES : (h + 1) * LANES] = part
    cm_ref[...] = jnp.where(alive, cm_ref[...], -1)

    sub_lo = iota((LANES, elems), 0)
    sub_hi = iota((groups, elems), 0)
    one_lo, one_hi = jnp.float32(1.0), jnp.float32(1.0)

    def corners(row_of, count):
        result = []
        for c in range(count):
            cols = []
            for h in range(halves):
                low = lo_ref[:, h * LANES : (h + 1) * LANES]
                high = hi_ref[:, h * LANES : (h + 1) * LANES]
                value = None
                for g in range(groups):
                    source = jnp.broadcast_to(row_of(c * groups + g), (ROWS, LANES))
                    got = pick(source, low)
                    value = got if value is None else jnp.where(high == g, got, value)
                cols.append(value)
            result.append(jnp.concatenate(cols, axis=1))
        return result

    def scatter(ys, counting=False):
        for c in range(3):
            y_high = ys[c].astype(BF16).astype(F32)
            y_ref[c * ROWS : (c + 1) * ROWS, :] = y_high
            y_ref[(3 + c) * ROWS : (4 + c) * ROWS, :] = ys[c] - y_high
        for a in range(basis):
            at = pl.ds(a * elems, elems)
            chosen = jnp.where(alive, hi_ref[a : a + 1, :], groups) == sub_hi
            for i in range(6):
                z_ref[i * groups : (i + 1) * groups, at] = jnp.where(
                    chosen, y_ref[i * ROWS + a : i * ROWS + a + 1, :], 0.0
                ).astype(BF16)
            if counting:
                z_ref[6 * groups : 7 * groups, at] = jnp.where(chosen, one_hi, 0.0).astype(BF16)
        rows = (7 if counting else 6) * groups
        both = mm_nt(z_ref[0:rows, :], b_ref[...])
        result = both[0 : 3 * groups] + both[3 * groups : 6 * groups]
        return (result, both[6 * groups :]) if counting else result

    s_low = jnp.broadcast_to(sent_nodes & (LANES - 1), (8, LANES))
    s_high = jnp.broadcast_to(sent_nodes >> 7, (8, LANES))

    def at_sent(sums):
        for c in range(3):
            for g in range(groups):
                r = c * groups + g
                s_ref[g * 8 + c : g * 8 + c + 1, :] = sums[r : r + 1, :]
        picked = jnp.zeros((8, LANES), F32)
        for g in range(groups):
            picked = jnp.where(s_high == g, pick(s_ref[g * 8 : g * 8 + 8, :], s_low), picked)
        return jnp.where(row < 3, picked, 0.0)

    def smoothed(near):
        return [mm3(smooth_parts, near[c]) for c in range(3)]

    def send_sums(sweep, value):
        v_send[sweep] = value
        for k in range(4):
            node_copy(sweep, k).start()

    near = []
    for c in range(3):
        near += corners(lambda r: x0_ref[c * groups + r : c * groups + r + 1, :], 1)
        for a in range(c * basis // 3, (c + 1) * basis // 3):
            at = pl.ds(a * elems, elems)
            b_ref[:, at] = jnp.where(sub_lo == lo_ref[a : a + 1, :], one_lo, 0.0).astype(BF16)
    sums, count = scatter(smoothed(near), True)
    first_sent = at_sent(sums)
    pl.semaphore_wait(barrier, len(greeted))
    send_sums(0, first_sent)

    for one in loads[6:]:
        one.wait()
    sent_elems = jnp.broadcast_to(flat(idx_ref[16:24, :], ghosts, 4), (8, LANES))
    sent_tile = [sent_elems]
    for t in range(1, tiles):
        sent_tile.append(pltpu.roll(sent_elems, ghosts * t, 1))
    first_of = [((slot_of + (slots - t)) & (slots - 1)) < 4 for t in range(tiles)]

    def choose(level, t, low, far):
        result = None
        for v in range(2 * t, min(2 * t + 2, fields)):
            got = None
            for h in range(halves):
                one = pick(u_ref[level, v * ROWS : (v + 1) * ROWS, h * LANES : (h + 1) * LANES], low)
                got = one if got is None else jnp.where(far == h, one, got)
            result = got if result is None else jnp.where(first_of[t], result, got)
        return result

    def send_ghosts(step):
        for k in range(4):
            tile = st_ref[step, 0]
            for t in range(1, tiles):
                tile = jnp.where(((slot_of + (slots - k)) & 3) == t, st_ref[step, t], tile)
            g_send[step, k] = tile
        for k in range(4):
            ghost_copy(step, k).start()

    got_lo, got_hi = got_nodes & (LANES - 1), got_nodes >> 7
    rb_ref[...] = jnp.where(iota((LANES, LANES), 0) == got_lo, one_lo, 0.0).astype(BF16)
    got_mask = iota((groups, LANES), 0) == got_hi
    count = count + mm_nt(jnp.where(got_mask, one_hi, 0.0).astype(BF16), rb_ref[...])
    half_inv = 0.5 / jnp.maximum(count, 1.0)
    hi_at_got = jnp.zeros((8, LANES), F32)
    got_lo8 = jnp.broadcast_to(got_lo, (8, LANES))
    got_hi8 = jnp.broadcast_to(got_hi, (8, LANES))
    for g in range(groups):
        hi_at_got = jnp.where(
            got_hi8 == g, pick(jnp.broadcast_to(half_inv[g : g + 1, :], (8, LANES)), got_lo8), hi_at_got
        )
    half_inv = jnp.concatenate([half_inv] * 3, axis=0)


    square = (LANES, LANES)
    got_row = jnp.broadcast_to(got_nodes, square)
    got_col = jnp.transpose(got_row)
    got_wide = jnp.concatenate([got_col] * halves, axis=1)
    for a in range(basis):
        node = cm_ref[a : a + 1, :]
        gr_ref[:, pl.ds(a * elems, elems)] = jnp.where(got_wide == node, one_lo, 0.0).astype(BF16)
    turned = jnp.transpose(pad_ref[0:LANES, :])[0:ROWS, :]
    for i in range(8):
        place = ka_ref if i < 4 else kb_ref
        placed = turned if i % 4 == 0 else pltpu.roll(turned, ROWS * (i % 4), 1)
        place[pl.ds(i, basis, stride=8), :] = placed[0:basis, :]
    k8_high, k8_low = split(jnp.concatenate([ka_ref[...], kb_ref[...]], axis=1))
    for pair in range(LANES // 16):
        both = []
        for part in range(2):
            for i in range(8):
                slot = pair * 16 + part * 8 + i
                node = sent_smem[slot // shared, slot % shared]
                oh_ref[part, i * ROWS : (i + 1) * ROWS, :] = jnp.where(
                    cm_ref[...] == node, one_lo, 0.0
                ).astype(BF16)
            both.append(mm(k8_high, oh_ref[part]) + mm(k8_low, oh_ref[part]))
        for b in range(basis):
            block = jnp.concatenate([one[b * 8 : (b + 1) * 8] for one in both], axis=0)
            high, low = split(block)
            at = pl.ds(b * elems, elems)
            hs_ref[pair * 16 : (pair + 1) * 16, at] = high
            hs_ref[LANES + pair * 16 : LANES + (pair + 1) * 16, at] = low
    response = mm_nt(hs_ref[...], gr_ref[...])
    response = split((response[0:LANES] + response[LANES:]) * hi_at_got[0:1, :])
    for i in range(2):
        tt_ref[i] = response[i]

    x_ref[...] = 0.5 * x0_ref[...] + sums * half_inv
    ahead = scatter(smoothed(corners(lambda r: x_ref[r : r + 1, :], 3)))
    ahead_sent = at_sent(ahead)

    def to_sent(arrived):
        high, low = split(arrived)
        return mm_nt(high, tt_ref[0]) + (mm_nt(low, tt_ref[0]) + mm_nt(high, tt_ref[1]))

    def prepare_slots():
        marked = jnp.where((got_col & (LANES - 1)) == iota(square, 1), iota(square, 0) + 1, 0)
        col_hi = got_col >> 7
        table = [
            jnp.max(jnp.where(col_hi == g, marked, 0), axis=0, keepdims=True) for g in range(groups)
        ]
        sl_ref[...] = corners(lambda r: table[r], 1)[0]

    def received(sweep):
        for k in range(4):
            node_copy(sweep, k).wait_recv()
        arrived = v_recv[sweep, 0]
        for k in range(1, 4):
            arrived = jnp.where(lane // shared == k, v_recv[sweep, k], arrived)
        return arrived

    same = jnp.where(got_row == got_col, one_lo, 0.0).astype(BF16)

    def gathered(arrived):
        high, low = split(arrived)
        spread = (mm(high, same) + mm(low, same)) * hi_at_got
        near = []
        for c in range(3):
            cols = []
            for h in range(halves):
                index = sl_ref[:, h * LANES : (h + 1) * LANES]
                source = jnp.broadcast_to(spread[c : c + 1, :], (ROWS, LANES))
                cols.append(jnp.where(index > 0, pick(source, (index + (LANES - 1)) & (LANES - 1)), 0.0))
            near.append(jnp.concatenate(cols, axis=1))
        return near

    def injected(arrived):
        arr_high = arrived.astype(BF16).astype(F32)
        arr_low = arrived - arr_high
        pieces = [
            jnp.where(got_mask, part[c : c + 1, :], 0.0).astype(BF16)
            for part in (arr_high, arr_low) for c in range(3)
        ]
        both = mm_nt(jnp.concatenate(pieces, axis=0), rb_ref[...])
        return (both[0 : 3 * groups] + both[3 * groups :]) * half_inv

    def prepare_weights():
        for i in range(faces + 1):
            matrix = stiff[...] if i == 0 else lift[i - 1]
            pad_ref[i * ROWS : i * ROWS + basis, 0:basis] = jnp.dot(
                mass_inv[...], matrix, precision=HIGHEST, preferred_element_type=F32
            )
        wide = []
        for first in range(0, faces + 1, 4):
            total = None
            for i in range(first, min(first + 4, faces + 1)):
                block = pad_ref[i * ROWS : (i + 1) * ROWS, :]
                if i > first:
                    block = pltpu.roll(block, ROWS * (i - first), 1)
                total = block if total is None else total + block
            wide.append(total)
        w_high, w_low = split(jnp.concatenate(wide, axis=1))
        w_ref[0:ROWS, :] = w_high
        w_ref[ROWS : 2 * ROWS, :] = w_low
        for c in range(3):
            fg_ref[0:faces, c * ROWS : c * ROWS + basis] = face_geo[:, c, :]

    def gather_local(step):
        for v in range(fields):
            for h in range(halves):
                for f in range(faces):
                    which = jnp.broadcast_to(neighbours[f, h : h + 1, :], (ROWS, LANES))
                    low, far = which & (LANES - 1), which >> 7
                    got = None
                    for s in range(halves):
                        other = pick(u_ref[step, v * ROWS : (v + 1) * ROWS, s * LANES : (s + 1) * LANES], low)
                        got = other if got is None else jnp.where(far == s, other, got)
                    r = (v * faces + f) * ROWS
                    nb_ref[r : r + ROWS, h * LANES : (h + 1) * LANES] = got

    def gather_sent(step):
        for t in range(tiles):
            for f in range(faces):
                which = jnp.broadcast_to(nbs_ref[t, f : f + 1, :], (ROWS, LANES))
                nl_ref[t, f] = choose(step, t, which & (LANES - 1), which >> 7)

    def wait_ghosts(step):
        for k in range(4):
            ghost_copy(step, k).wait_recv()
        for t in range(tiles):
            tile = g_recv[step, 0]
            for k in range(1, 4):
                tile = jnp.where(((slot_of + (slots - t)) & 3) == k, g_recv[step, k], tile)
            gt_ref[t] = tile

    depth = (faces + 1) * ROWS

    def times(stack):
        high, low = split(jnp.concatenate(stack, axis=0))
        first = mm(w_ref[:, 0:depth], high)
        return first[0:ROWS] + (first[ROWS:] + mm(w_ref[0:ROWS, 0:depth], low))

    def prepare_sent():
        for f in range(faces):
            cols = []
            for t in range(tiles):
                cols.append(neighbour_of_sent(0, t, f) - st_ref[0, t])
            ds_ref[f + 1] = one_face(f + 1, jnp.concatenate(cols, axis=1))
        ds_ref[0] = one_face(0, jnp.concatenate([st_ref[0, t] for t in range(tiles)], axis=1))

    def one_face(i, value):
        at = i * ROWS
        return mm3((w_ref[0:ROWS, at : at + ROWS], w_ref[ROWS : 2 * ROWS, at : at + ROWS]), value)

    def kept_sent(t):
        return jnp.where(sent_tile[t][0:1, :] < live[0], 1.0, 0.0)

    def first_sent_step():
        for t in range(tiles):
            at = pl.ds(t * LANES, LANES)
            new = ds_ref[0, :, at]
            for f in range(faces):
                new = new + rs_ref[t, f : f + 1, :] * ds_ref[f + 1, :, at]
            st_ref[1, t] = new * kept_sent(t)

    def neighbour_of_sent(step, t, f):
        which = jnp.broadcast_to(nbs_ref[t, f : f + 1, :], (ROWS, LANES))
        at = which + jnp.where(first_of[t], ghosts * t, ghosts * (t + 4))
        return jnp.where(which >= elems, pick(gt_ref[t], at & (LANES - 1)), nl_ref[t, f])

    def advance_sent(step):
        stack = [jnp.concatenate([st_ref[step, t] for t in range(tiles)], axis=1)]
        for f in range(faces):
            cols = []
            for t in range(tiles):
                got = neighbour_of_sent(step, t, f)
                cols.append(rs_ref[t, f : f + 1, :] * (got - st_ref[step, t]))
            stack.append(jnp.concatenate(cols, axis=1))
        new = times(stack)
        for t in range(tiles):
            st_ref[step + 1, t] = new[:, t * LANES : (t + 1) * LANES] * kept_sent(t)

    def change_of(v, step):
        u = u_ref[step, v * ROWS : (v + 1) * ROWS, :]
        stack = [u]
        for f in range(faces):
            cols = []
            r = (v * faces + f) * ROWS
            for h in range(halves):
                which = jnp.broadcast_to(neighbours[f, h : h + 1, :], (ROWS, LANES))
                got = pick(gt_ref[v // 2], (which + ghosts * (v // 2 + 4 * (v % 2))) & (LANES - 1))
                cols.append(jnp.where(which >= elems, got, nb_ref[r : r + ROWS, h * LANES : (h + 1) * LANES]))
            stack.append(rate_ref[f : f + 1, :] * (jnp.concatenate(cols, axis=1) - u))
        return times(stack)

    def finish_round(r, most):
        at = sum(len(p) for p in partners[:r])
        tile = m_send[r]
        for j in range(len(partners[r])):
            most_copy(r, j).wait_recv()
            tile = jnp.maximum(tile, m_recv[at + j])
        most = tile[0:1, 0:1]
        if r + 1 < len(partners):
            m_send[r + 1] = jnp.broadcast_to(most, (1, LANES))
            for j in range(len(partners[r + 1])):
                most_copy(r + 1, j).start()
        return most

    for sweep in range(SWEEPS - 1):
        arrived = received(sweep)
        send_sums(sweep + 1, ahead_sent + to_sent(arrived))
        if sweep == 0:
            for v in range(fields):
                for h in range(halves):
                    u_ref[0, v * ROWS : v * ROWS + basis, h * LANES : (h + 1) * LANES] = states[
                        v * basis : (v + 1) * basis, h, :
                    ]
            for t in range(tiles):
                which = jnp.broadcast_to(sent_tile[t][0:1, :], (ROWS, LANES))
                st_ref[0, t] = choose(0, t, which & (LANES - 1), which >> 7)
            send_ghosts(0)
            prepare_slots()
        ys = smoothed(gathered(arrived))
        x_ref[...] = x_ref[...] + injected(arrived)
        sums = ahead + scatter(ys)
        x_ref[...] = 0.5 * x_ref[...] + sums * half_inv
        if sweep < SWEEPS - 2:
            ahead = scatter(smoothed(corners(lambda r: x_ref[r : r + 1, :], 3)))
            ahead_sent = at_sent(ahead)

    prepare_weights()
    geo_parts = split(fg_ref[:, 0 : 3 * ROWS])
    mv_ref[...] = x_ref[...] - x0_ref[...]
    projected = mm3(geo_parts, jnp.concatenate(corners(lambda r: mv_ref[r : r + 1, :], 3), axis=0))
    base = jnp.concatenate([rates[:, h, :] for h in range(halves)], axis=1)
    keep = jnp.where(alive, 1.0, 0.0)
    for t in range(tiles):
        low, far = sent_tile[t] & (LANES - 1), sent_tile[t] >> 7
        got = jnp.zeros((8, LANES), jnp.int32)
        for h in range(halves):
            nbp_ref[0:faces, :] = neighbours[:, h, :]
            got = jnp.where(far == h, pick(nbp_ref[...], low), got)
        nbs_ref[t] = got
    gather_sent(0)
    gather_local(0)
    wait_ghosts(0)
    prepare_sent()

    arrived = received(SWEEPS - 1)
    near = gathered(arrived)
    projected = projected + mm3(geo_parts, jnp.concatenate(near, axis=0))
    rate = base * (1.0 + 0.5 * jnp.tanh(projected[0:faces])) * keep
    rate_ref[0:faces, :] = rate
    for t in range(tiles):
        low, far = sent_tile[t] & (LANES - 1), sent_tile[t] >> 7
        got = jnp.zeros((8, LANES), F32)
        for h in range(halves):
            got = jnp.where(far == h, pick(rate_ref[:, h * LANES : (h + 1) * LANES], low), got)
        rs_ref[t] = got
    first_sent_step()
    send_ghosts(1)
    most = jnp.max(jnp.sum(rate, axis=0, keepdims=True), axis=1, keepdims=True)
    m_send[0] = jnp.broadcast_to(most, (1, LANES))
    for j in range(len(partners[0]) if rounds else 0):
        most_copy(0, j).start()
    out_c[...] = x_ref[...] + injected(arrived)

    for step in range(STEPS - 1):
        for v in range(fields):
            u_ref[step + 1, v * ROWS : (v + 1) * ROWS, :] = keep * change_of(v, step)
        if step + 2 < STEPS:
            gather_sent(step + 1)
        gather_local(step + 1)
        if step == STEPS - 2:
            for r in range(step, len(partners)):
                most = finish_round(r, most)
            scale = jnp.broadcast_to(CFL / most, (ROWS, elems))
            for v in range(fields):
                total = math.comb(STEPS, STEPS - 1) * u_ref[STEPS - 1, v * ROWS : (v + 1) * ROWS, :]
                for k in range(STEPS - 2, -1, -1):
                    total = math.comb(STEPS, k) * u_ref[k, v * ROWS : (v + 1) * ROWS, :] + scale * total
                u_ref[STEPS, v * ROWS : (v + 1) * ROWS, :] = total
        wait_ghosts(step + 1)
        if step + 2 < STEPS:
            advance_sent(step + 1)
            send_ghosts(step + 2)
        if step < min(STEPS - 2, len(partners)):
            most = finish_round(step, most)
    scale = keep * (scale * scale) * (scale * scale)
    for v in range(fields):
        new = u_ref[STEPS, v * ROWS : (v + 1) * ROWS, :] + scale * change_of(v, STEPS - 1)
        for h in range(halves):
            out_u[v * basis : (v + 1) * basis, h, :] = new[0:basis, h * LANES : (h + 1) * LANES]

    for sweep in range(SWEEPS):
        for k in range(4):
            node_copy(sweep, k).wait_send()
    for step in range(STEPS):
        for k in range(4):
            ghost_copy(step, k).wait_send()
    for r, one in enumerate(partners):
        for j in range(len(one)):
            most_copy(r, j).wait_send()


def hand_over(coords, remapped, out_c, out_u, sem):
    moves = [
        pltpu.make_async_copy(remapped, out_u, sem.at[0]),
        pltpu.make_async_copy(coords, out_c, sem.at[1]),
    ]
    for one in moves:
        one.start()
    for one in moves:
        one.wait()


def on_device(*args):
    pos, states, conn = args[:3]
    parts = lax.axis_size("dom")
    w = max(parts // 8, 1)
    shifts = (1, -1, w, -w)
    rounds = rounds_of(parts)
    total = sum(r - 1 for r, _ in rounds)
    basis, elems = conn.shape[1:]
    fields, faces = states.shape[1], args[6].shape[1]
    groups = pos.shape[2] // LANES
    nodes = pos.shape[2]
    halves = elems // LANES
    tiles = (fields + 1) // 2
    flat = list(args)
    for i, rows in ((0, 3 * groups), (1, fields * basis * halves), (2, basis * halves), (6, faces * halves), (10, faces * halves)):
        flat[i] = args[i].reshape(rows, LANES) if i == 0 else args[i].reshape(rows // halves, halves, LANES)
    for i in (3, 4, 5):
        flat[i] = args[i][0]
    vmem = pl.BlockSpec(memory_space=pltpu.VMEM)
    smem = pl.BlockSpec(memory_space=pltpu.SMEM)
    hbm = pl.BlockSpec(memory_space=pl.ANY)
    specs = [smem if i == 7 else hbm for i in range(len(args))]
    held = [pltpu.VMEM(a.shape, a.dtype) for i, a in enumerate(flat) if i != 7]
    held.append(pltpu.SMEM(flat[3].shape, flat[3].dtype))
    scratch = held + [
        pltpu.SemaphoreType.DMA((len(held),)),
        pltpu.VMEM((3 * groups, LANES), F32),
        pltpu.VMEM((8 * groups, LANES), F32),
        pltpu.VMEM((ROWS, elems), jnp.int32),
        pltpu.VMEM((ROWS, elems), jnp.int32),
        pltpu.VMEM((6 * ROWS, elems), F32),
        pltpu.VMEM((7 * groups, basis * elems), BF16),
        pltpu.VMEM((LANES, basis * elems), BF16),
        pltpu.VMEM((LANES, LANES), BF16),
        pltpu.VMEM((STEPS + 1, fields * ROWS, elems), F32),
        pltpu.VMEM((fields * faces * ROWS, elems), F32),
        pltpu.VMEM((8, elems), F32),
        pltpu.VMEM(((faces + 1) * ROWS, LANES), F32),
        pltpu.VMEM((8, LANES), F32),
        pltpu.VMEM((2 * ROWS, 2 * LANES), BF16),
        pltpu.VMEM((24, LANES), jnp.int32),
        pltpu.VMEM((3 * groups, LANES), F32),
        pltpu.VMEM((ROWS, elems), jnp.int32),
        pltpu.VMEM((basis * 8, LANES), F32),
        pltpu.VMEM((basis * 8, LANES), F32),
        pltpu.VMEM((2, 8 * ROWS, elems), BF16),
        pltpu.VMEM((2 * LANES, basis * elems), BF16),
        pltpu.VMEM((LANES, basis * elems), BF16),
        pltpu.VMEM((2, LANES, LANES), BF16),
        pltpu.VMEM((ROWS, elems), jnp.int32),
        pltpu.VMEM((STEPS, tiles, ROWS, LANES), F32),
        pltpu.VMEM((tiles, ROWS, LANES), F32),
        pltpu.VMEM((tiles, faces, ROWS, LANES), F32),
        pltpu.VMEM((tiles, 8, LANES), jnp.int32),
        pltpu.VMEM((tiles, 8, LANES), F32),
        pltpu.VMEM((8, LANES), jnp.int32),
        pltpu.VMEM((faces + 1, ROWS, tiles * LANES), F32),
        pltpu.VMEM((SWEEPS, 8, LANES), F32),
        pltpu.VMEM((SWEEPS, 4, 8, LANES), F32),
        pltpu.VMEM((STEPS, 4, ROWS, LANES), F32),
        pltpu.VMEM((STEPS, 4, ROWS, LANES), F32),
        pltpu.VMEM((max(len(rounds), 1), 1, LANES), F32),
        pltpu.VMEM((max(total, 1), 1, LANES), F32),
        pltpu.SemaphoreType.DMA((SWEEPS, 4)),
        pltpu.SemaphoreType.DMA((SWEEPS, 4)),
        pltpu.SemaphoreType.DMA((STEPS, 4)),
        pltpu.SemaphoreType.DMA((STEPS, 4)),
        pltpu.SemaphoreType.DMA((max(total, 1),)),
        pltpu.SemaphoreType.DMA((max(total, 1),)),
    ]
    coords, remapped = pl.pallas_call(
        functools.partial(kernel, parts, shifts, rounds, basis, elems, fields, faces, nodes),
        out_shape=(
            jax.ShapeDtypeStruct((3 * groups, LANES), F32),
            jax.ShapeDtypeStruct((fields * basis, halves, LANES), F32),
        ),
        in_specs=specs,
        out_specs=(vmem, vmem),
        scratch_shapes=scratch,
        compiler_params=pltpu.CompilerParams(
            collective_id=0, has_side_effects=True, vmem_limit_bytes=32 * 1024 * 1024
        ),
    )(*[a if i == 7 else pltpu.with_memory_space_constraint(a, pltpu.HBM) for i, a in enumerate(flat)])
    coords, remapped = pl.pallas_call(
        hand_over,
        out_shape=(pltpu.HBM(coords.shape, F32), pltpu.HBM(remapped.shape, F32)),
        in_specs=[vmem, vmem],
        out_specs=(hbm, hbm),
        scratch_shapes=[pltpu.SemaphoreType.DMA((2,))],
        compiler_params=pltpu.CompilerParams(vmem_limit_bytes=1024 * 1024),
    )(coords, remapped)
    return coords.reshape(pos.shape), remapped.reshape(states.shape)


def solution(mesh):
    dom = lambda rank: P("dom", *([None] * (rank - 1)))
    in_specs = (
        dom(3), dom(4), dom(3), dom(3), dom(3), dom(3), dom(3), P("dom"),
        P(), P(), dom(3), P(), P(), P(),
    )
    return jax.shard_map(
        on_device, mesh=mesh, in_specs=in_specs, out_specs=(dom(3), dom(4)), check_vma=False
    )
```
